256 devices in a mesh: dp: 16 (over y_hi, x, core), fsdp: 16 (over z, y_lo).
Axes of the slice: x: 4, y: 4 (y_hi: 2, y_lo: 2; y = y_hi * 2 + y_lo), z: 8, core: 2. Of those that a mesh axis runs over, the one named last changes fastest.
Arguments:
- cotangent: bfloat16 [32768, 2560], P(('dp', 'fsdp')), may hold values from -6 to 6
- out_weight: bfloat16 [1280, 2560], P('fsdp'), may hold values from -0.15625 to 0.15625
- queries: bfloat16 [49152, 1280], P(('dp', 'fsdp')), may hold values from -200 to 200
- key_vectors: bfloat16 [49152, 1280], P(('dp', 'fsdp')), may hold values from -5 to 5
- value_vectors: bfloat16 [49152, 1280], P(('dp', 'fsdp')), may hold values from -6 to 6
- destination: int32 [32768], P(('dp', 'fsdp')), may hold values from 0 to 3071, as said below
- protein_ids: int32 [49152], P(('dp', 'fsdp')), may hold values from -192 to 79, as said below
Outputs:
- query_grad: bfloat16 [49152, 1280], P(('dp', 'fsdp'))
- key_grad: bfloat16 [49152, 1280], P(('dp', 'fsdp'))
- value_grad: bfloat16 [49152, 1280], P(('dp', 'fsdp'))
- weight_grad: float32 [1280, 2560], P('fsdp')
The draws below stay inside these ranges and needn't reach their ends.
Inputs may be any that keep to these rules, and one draw needn't show every extreme that they name: `destination`: in each fsdp group every owner uses a prefix of its 192 slots and each used slot is named by exactly one token row of the group; at most 12 rows of one device go to one owner, and in every group the last owner uses all 192 slots and receives exactly 12 rows from every device. `protein_ids`: used slots of owner o hold ids 5 * o to 5 * o + 4, in contiguous runs; unused slot s of an owner holds -1 - s; in every group the last owner holds 5 proteins.
All inputs are finite; a program needn't handle non-finite values.
Results may differ from the reference program's by a relative error of at most 0.0058.
Values may be sent and summed in bfloat16 or wider, within the bound.
A program may use at most 128 MiB of HBM per device.

```python
import math
import jax
import jax.numpy as jnp
from jax import lax

D = 2560
HEADS = 20
HEAD = 64
TOK_DEV = 128
HW = 1280
OWN = 192
N_DP = 16
N_FSDP = 16


def layout_tables(key):

    def one_group(group_key):
        load_key, pick_key, order_key, shuffle_key, jitter_key = jax.random.split(group_key, 5)
        pair_count = N_FSDP // 2
        excess = jax.random.randint(load_key, (pair_count,), 0, TOK_DEV // 2 + 1)
        forced = jax.random.randint(pick_key, (), 0, pair_count)
        excess = jnp.where(jnp.arange(pair_count) == forced, TOK_DEV // 2, excess)
        shuffled_loads = jax.random.permutation(order_key, jnp.concatenate([TOK_DEV + excess, TOK_DEV - excess]))
        fullest = jnp.argmax(shuffled_loads)
        owner_loads = shuffled_loads.at[fullest].set(shuffled_loads[N_FSDP - 1]).at[N_FSDP - 1].set(OWN)
        range_ends = jnp.cumsum(owner_loads)
        range_starts = range_ends - owner_loads
        group_rows = jnp.arange(N_FSDP * TOK_DEV)
        owner_of = jnp.sum(group_rows[:, None] >= range_ends[None, :], axis=1)
        slot_of = group_rows - range_starts[owner_of]
        device_of = group_rows % N_FSDP
        row_in_device = group_rows // N_FSDP
        shuffles = jax.vmap(lambda one_key: jax.random.permutation(one_key, TOK_DEV))(jax.random.split(shuffle_key, N_FSDP))
        placed_at = device_of * TOK_DEV + shuffles[device_of, row_in_device]
        targets = jnp.zeros((N_FSDP * TOK_DEV,), jnp.int32).at[placed_at].set((owner_of * OWN + slot_of).astype(jnp.int32))
        protein_count = 1 + owner_loads * owner_loads // (TOK_DEV * TOK_DEV // 2)
        jitter_width = owner_loads // (4 * protein_count)
        raw_bits = jax.random.randint(jitter_key, (N_FSDP, 4), 0, 1 << 20)
        jitter = raw_bits % (2 * jitter_width[:, None] + 1) - jitter_width[:, None]
        cut_numbers = jnp.arange(1, 5)
        bounds = cut_numbers[None, :] * owner_loads[:, None] // protein_count[:, None] + jitter
        slot_numbers = jnp.arange(OWN)
        active = cut_numbers[None, :] < protein_count[:, None]
        within = jnp.sum((slot_numbers[None, None, :] >= bounds[:, :, None]) & active[:, :, None], axis=1)
        owners = jnp.arange(N_FSDP)
        slot_ids = jnp.where(slot_numbers[None, :] < owner_loads[:, None], owners[:, None] * 5 + within, -1 - slot_numbers[None, :])
        return (targets, slot_ids.reshape(-1).astype(jnp.int32))
    group_keys = jax.vmap(lambda number: jax.random.fold_in(key, number))(jnp.arange(N_DP))
    targets, slot_ids = jax.vmap(one_group)(group_keys)
    return (targets.reshape(-1), slot_ids.reshape(-1))


def base_vectors(key):
    return jnp.clip(jax.random.normal(jax.random.fold_in(key, 7919), (N_DP * N_FSDP * OWN, HEADS * HEAD), jnp.float32), -5.0, 5.0)


def draw_destination(key, part):
    tables = layout_tables(key)
    return tables[0]


def draw_protein_ids(key, part):
    tables = layout_tables(key)
    return tables[1]


def draw_key_vectors(key, part):
    common = base_vectors(key)
    return common.astype(jnp.bfloat16)


def draw_queries(key, part):
    common = base_vectors(key)
    key = jax.random.fold_in(key, 37)
    fresh = jnp.clip(jax.random.normal(key, common.shape, jnp.float32), -5.0, 5.0)
    return fresh.astype(jnp.bfloat16)


def shard_levels(key, extent, shards, smallest, high):
    level, own = 1.0, jax.random.fold_in(key, 6)
    for axis_at, blocks in shards:
        heights = jnp.exp(jax.random.uniform(jax.random.fold_in(own, axis_at), (blocks,), jnp.float32, smallest / len(shards), high / len(shards)))
        level = level * jnp.repeat(heights, extent[axis_at] // blocks).reshape([-1 if axis == axis_at else 1 for axis in range(len(extent))])
    return level


def scatter_about(rng, shape, deviation, bound, cuts=(), held_as=jnp.bfloat16):
    result = jax.random.normal(rng, shape, jnp.float32) * deviation
    if len(cuts) > 0:
        result = shard_levels(rng, shape, cuts, -0.22, 0.18) * result
    return jnp.clip(result, min=-bound, max=bound).astype(held_as)


def setup_inputs(seed: int = 0) -> dict:
    key_of = jax.random.split(jax.random.key(seed), 8)
    return {
        "cotangent": scatter_about(key_of[0], (N_DP * N_FSDP * TOK_DEV, D), 0.7, 6.0, ((0, 256),)),
        "out_weight": scatter_about(key_of[1], (HW, D), HW ** -0.5, 0.15625, ((0, 16),)),
        "queries": draw_queries(jax.random.fold_in(key_of[7], 71), 0),
        "key_vectors": draw_key_vectors(jax.random.fold_in(key_of[7], 71), 0),
        "value_vectors": scatter_about(key_of[4], (N_DP * N_FSDP * OWN, HW), 1.0, 6.0, ((0, 256),)),
        "destination": draw_destination(jax.random.fold_in(key_of[7], 71), 0),
        "protein_ids": draw_protein_ids(jax.random.fold_in(key_of[7], 71), 0),
    }


def heads_of(matrix, col_begin):
    return matrix[:, col_begin:col_begin + 5 * HEAD].reshape(matrix.shape[0], 5, HEAD).astype(jnp.float32)

def owner_backward(query_rows, key_rows, value_rows, grad_rows, slot_ids):
    row_count = query_rows.shape[0]
    same_protein = slot_ids[:, None] == slot_ids[None, :]
    live_rows = (slot_ids >= 0)[:, None]
    score_scale = 1.0 / math.sqrt(HEAD)
    query_parts, key_parts, value_parts, attended_parts = ([], [], [], [])
    for head_first in range(0, HEADS, 5):
        col_begin = head_first * HEAD
        query_part = heads_of(query_rows, col_begin)
        key_part = heads_of(key_rows, col_begin)
        value_part = heads_of(value_rows, col_begin)
        grad_part = heads_of(grad_rows, col_begin)
        scores = jnp.einsum('qhd,khd->hqk', query_part, key_part) * score_scale
        scores = jnp.where(same_protein[None], scores, -1e+30)
        row_max = lax.optimization_barrier(jnp.max(scores, axis=2, keepdims=True))
        exponent = jnp.exp(scores - row_max)
        softmax = exponent / lax.optimization_barrier(jnp.sum(exponent, axis=2, keepdims=True))
        rounded = lax.optimization_barrier(softmax.astype(jnp.bfloat16)).astype(jnp.float32)
        attended = jnp.einsum('hqk,khd->qhd', rounded, value_part)
        value_grad = jnp.einsum('hqk,qhd->khd', rounded, grad_part)
        prob_grad = jnp.einsum('qhd,khd->hqk', grad_part, value_part)
        delta = lax.optimization_barrier(jnp.sum(softmax * prob_grad, axis=2, keepdims=True))
        score_grad = lax.optimization_barrier((softmax * (prob_grad - delta)).astype(jnp.bfloat16)).astype(jnp.float32)
        query_grad = jnp.einsum('hqk,khd->qhd', score_grad, key_part) * score_scale
        key_grad = jnp.einsum('hqk,qhd->khd', score_grad, query_part) * score_scale
        query_parts.append(query_grad.reshape(row_count, 5 * HEAD))
        key_parts.append(key_grad.reshape(row_count, 5 * HEAD))
        value_parts.append(value_grad.reshape(row_count, 5 * HEAD))
        attended_parts.append(attended.reshape(row_count, 5 * HEAD))
    query_all = jnp.where(live_rows, jnp.concatenate(query_parts, axis=1), 0.0).astype(jnp.bfloat16)
    key_all = jnp.where(live_rows, jnp.concatenate(key_parts, axis=1), 0.0).astype(jnp.bfloat16)
    value_all = jnp.where(live_rows, jnp.concatenate(value_parts, axis=1), 0.0).astype(jnp.bfloat16)
    attended_all = jnp.concatenate(attended_parts, axis=1).astype(jnp.bfloat16)
    return (query_all, key_all, value_all, attended_all)

def reference(cotangent, out_weight, queries, key_vectors, value_vectors, destination, protein_ids):
    group_rows = N_FSDP * TOK_DEV
    group_slots = N_FSDP * OWN
    width = HEADS * HEAD

    def one_group(group_index):
        token_first = (group_index * group_rows).astype(jnp.int32)
        slot_first = (group_index * group_slots).astype(jnp.int32)
        grad_rows = lax.dynamic_slice_in_dim(cotangent, token_first, group_rows, 0)
        targets = lax.dynamic_slice_in_dim(destination, token_first, group_rows, 0)
        query_rows = lax.dynamic_slice_in_dim(queries, slot_first, group_slots, 0)
        key_rows = lax.dynamic_slice_in_dim(key_vectors, slot_first, group_slots, 0)
        value_rows = lax.dynamic_slice_in_dim(value_vectors, slot_first, group_slots, 0)
        slot_ids = lax.dynamic_slice_in_dim(protein_ids, slot_first, group_slots, 0)
        out_grad = jnp.dot(grad_rows, out_weight.T, preferred_element_type=jnp.float32).astype(jnp.bfloat16)
        slot_grad = jnp.zeros((group_slots, width), jnp.bfloat16).at[targets].set(out_grad)

        def per_owner(owner_index):
            first = (owner_index * OWN).astype(jnp.int32)
            return owner_backward(lax.dynamic_slice_in_dim(query_rows, first, OWN, 0), lax.dynamic_slice_in_dim(key_rows, first, OWN, 0), lax.dynamic_slice_in_dim(value_rows, first, OWN, 0), lax.dynamic_slice_in_dim(slot_grad, first, OWN, 0), lax.dynamic_slice_in_dim(slot_ids, first, OWN, 0))
        query_all, key_all, value_all, attended_all = lax.map(per_owner, jnp.arange(N_FSDP, dtype=jnp.int32))
        attended_flat = attended_all.reshape(group_slots, width)
        token_out = attended_flat[targets]
        partial_value = jnp.dot(token_out.T, grad_rows, preferred_element_type=jnp.float32)
        return (query_all.reshape(group_slots, width), key_all.reshape(group_slots, width), value_all.reshape(group_slots, width), partial_value)
    query_grad, key_grad, value_grad, partials = lax.map(one_group, jnp.arange(N_DP, dtype=jnp.int32))
    return (query_grad.reshape(-1, width), key_grad.reshape(-1, width), value_grad.reshape(-1, width), lax.optimization_barrier(jnp.sum(partials, axis=0)))
```

```python
import jax
import jax.numpy as jnp
from jax import lax
from jax.experimental import pallas as pl
from jax.experimental.pallas import tpu as pltpu
from jax.sharding import PartitionSpec as P

F32 = jnp.float32
BF16 = jnp.bfloat16
MESH = pl.DeviceIdType.MESH

NX, NY, NZ, NF = 4, 4, 8, 16
TOK = 128
OWN = 192
CAP = 12
D = 2560
QD = D // 4
ROWS = 80
PAIRS = 10
SCALE = 0.125


def fdiv(values, by):
    return jnp.floor((values + 0.5) * (1.0 / by))


def iota(shape, dim):
    return lax.broadcasted_iota(jnp.int32, shape, dim).astype(F32)


def dot_nt(a, b):
    return lax.dot_general(a, b, (((1,), (1,)), ((), ())), preferred_element_type=F32)


def dot_tn(a, b):
    return lax.dot_general(a, b, (((0,), (0,)), ((), ())), preferred_element_type=F32)


def dot_nn(a, b):
    return jnp.dot(a, b, preferred_element_type=F32)


def row_of(y, j):
    return 4 * (y // 2) + 2 * j + y % 2


def kernel(
    cot_hbm, w_hbm, q_hbm, k_hbm, v_hbm, dest_ref, ids_ref,
    dq_hbm, dk_hbm, dv_hbm, wg_hbm,
    cot_v, q_v, k_v, v_v, dq_v, dk_v, dv_v,
    dsend, drecv, packed, arrived, c_all,
    att, att_all, att_t, probs, same_v,
    w0, w1, g_tmp, g_v,
    s0, s1, r0, r1, t0, t1, u0, u1, vf, vb, zr, fall,
    load_sem, out_sem, wg_sem, own_sem,
    d_ssem, d_rsem, c_ssem, c_rsem,
    az_ssem, az_rsem, a1_ssem, a1_rsem, a2_ssem, a2_rsem,
    sib_ssem, sib_rsem,
    b2_ssem, b2_rsem, b1_ssem, b1_rsem, bz_ssem, bz_rsem,
    f1_ssem, f1_rsem, f2_ssem, f2_rsem, f3_ssem, f3_rsem,
):
    dp = lax.axis_index("dp")
    f = lax.axis_index("fsdp")
    c = dp % 2
    x = (dp // 2) % NX
    h = dp // 8
    z = f // 2
    y = 2 * h + f % 2

    def dev(x_, y_, z_, c_):
        return (((y_ // 2) * NX + x_) * 2 + c_, z_ * 2 + y_ % 2)

    def rcopy(src, dst, ssem, rsem, target):
        return pltpu.make_async_remote_copy(
            src_ref=src, dst_ref=dst, send_sem=ssem, recv_sem=rsem,
            device_id=target, device_id_type=MESH,
        )

    sibling = dev(x, y, z, 1 - c)

    loads = [
        pltpu.make_async_copy(src, dst, load_sem.at[i])
        for i, (src, dst) in enumerate(
            ((cot_hbm, cot_v), (q_hbm, q_v), (k_hbm, k_v), (v_hbm, v_v))
        )
    ]
    for load in loads:
        load.start()

    barrier = pltpu.get_barrier_semaphore()

    @pl.loop(1, NF)
    def _(s):
        pl.semaphore_signal(
            barrier, inc=1, device_id=(dp, (f + s) % NF), device_id_type=MESH
        )

    for s in range(1, 4):
        pl.semaphore_signal(
            barrier, inc=1, device_id=dev((x + s) % NX, y, z, c), device_id_type=MESH
        )
        pl.semaphore_signal(
            barrier, inc=1, device_id=dev(x, (y + s) % NY, z, c), device_id_type=MESH
        )
    pl.semaphore_signal(barrier, inc=1, device_id=sibling, device_id_type=MESH)
    pl.semaphore_wait(barrier, 22)

    active = z // 4 == c
    root = jnp.logical_and(active, (z % 4) // 2 == h)
    w_mine = w_hbm.at[:, pl.ds(pl.multiple_of(x * QD, 128), QD)]

    def spread_z(dst):
        pltpu.make_async_copy(w_mine, dst, own_sem).start()

        @pl.loop(1, NZ)
        def _(s):
            rcopy(
                w_mine, dst, az_ssem.at[s], az_rsem.at[z % 2], dev(x, y, (z + s) % NZ, c)
            ).start()

    w0_mine = w0.at[x, y]
    w1_mine = w1.at[y, x]

    @pl.when(jnp.logical_and(root, z % 2 == 0))
    def _():
        spread_z(w0_mine)

    @pl.when(jnp.logical_and(root, z % 2 == 1))
    def _():
        spread_z(w1_mine)

    dest = dest_ref[...]
    dsend[...] = jnp.broadcast_to(dest, (8, TOK))

    @pl.loop(1, NF)
    def _(s):
        rcopy(dsend, drecv.at[f], d_ssem.at[s], d_rsem.at[f], (dp, (f + s) % NF)).start()

    drecv[f] = dsend[...]

    dest_f = dest.astype(F32)
    owner = fdiv(dest_f, OWN)
    row_i = iota((TOK, TOK), 0)
    col_i = iota((TOK, TOK), 1)
    owner_col = jnp.sum(
        jnp.where(row_i == col_i, jnp.broadcast_to(owner, (TOK, TOK)), 0.0),
        axis=1, keepdims=True,
    )
    ahead = jnp.where(jnp.logical_and(owner_col == owner, row_i < col_i), 1.0, 0.0)
    position = owner * CAP + jnp.sum(ahead, axis=0, keepdims=True)
    p_col = iota((NF * 4 * CAP, 1), 0)
    p_owner = fdiv(p_col, 4 * CAP)
    p_in = p_col - p_owner * (4 * CAP)
    p_quarter = fdiv(p_in, CAP)
    p_rank = p_in - p_quarter * CAP
    p_pos = p_owner * CAP + p_rank
    picks = jnp.concatenate(
        [
            jnp.where(jnp.where(p_quarter == k, p_pos, -1.0) == position, 1.0, 0.0).astype(BF16)
            for k in range(4)
        ],
        axis=1,
    )
    loads[0].wait()
    stacked = jnp.concatenate([cot_v[:, QD * k : QD * (k + 1)] for k in range(4)], axis=0)
    packed[...] = dot_nn(picks, stacked).astype(BF16).reshape(NF, 4 * CAP, QD)

    @pl.loop(1, NF)
    def _(s):
        to = (f + s) % NF
        rcopy(packed.at[to], arrived.at[f], c_ssem.at[s], c_rsem.at[f], (dp, to)).start()

    arrived[f] = packed[f]

    @pl.when(root)
    def _():
        pltpu.make_async_copy(w_mine, w0_mine, own_sem).wait()

    @pl.when(z != 4 * c + 2 * h)
    def _():
        rcopy(w0_mine, w0_mine, az_ssem.at[0], az_rsem.at[0], sibling).wait_recv()

    for s in range(1, 4):
        rcopy(
            w0_mine, w0_mine, a1_ssem.at[0, s], a1_rsem.at[0, y], dev(x, (y + s) % NY, z, c)
        ).start()

    @pl.when(z != 4 * c + 2 * h + 1)
    def _():
        rcopy(w1_mine, w1_mine, az_ssem.at[0], az_rsem.at[1], sibling).wait_recv()

    for s in range(1, 4):
        rcopy(
            w1_mine, w1_mine, a1_ssem.at[1, s], a1_rsem.at[1, x], dev((x + s) % NX, y, z, c)
        ).start()

    for load in loads[1:]:
        load.wait()
    ids = ids_ref[...].astype(F32)
    srow = iota((OWN, OWN), 0)
    scol = iota((OWN, OWN), 1)
    ids_col = jnp.sum(
        jnp.where(srow == scol, jnp.broadcast_to(ids, (OWN, OWN)), 0.0), axis=1, keepdims=True
    )
    same_v[...] = jnp.where(ids_col == ids, 0.0, -1e30)
    lane = lax.broadcasted_iota(jnp.int32, (1, 128), 1)
    head_masks = (
        jnp.where(lane < 64, 1.0, 0.0).astype(BF16),
        jnp.where(lane < 64, 0.0, 1.0).astype(BF16),
    )
    first_head = lax.broadcasted_iota(jnp.int32, (OWN, 128), 1) < 64

    def forward(p):
        at = pl.ds(pl.multiple_of(p * 128, 128), 128)
        qp, kp, vp = q_v[:, at], k_v[:, at], v_v[:, at]
        outs = []
        for i in range(2):
            scores = dot_nt(qp * head_masks[i], kp) * SCALE
            scores = jnp.where(same_v[...] == 0.0, scores, -1e30)
            top = jnp.max(scores, axis=1, keepdims=True)
            e = jnp.exp(scores - top)
            prob = e * (1.0 / jnp.sum(e, axis=1, keepdims=True))
            probs[2 * p + i] = prob
            outs.append(dot_nn(prob.astype(BF16), vp))
        att[p] = jnp.where(first_head, outs[0], outs[1]).astype(BF16)

    pl.loop(0, PAIRS // 2)(forward)

    for s in range(1, 4):
        ys = (y + s) % NY
        rcopy(w0.at[x, ys], w0.at[x, ys], a1_ssem.at[0, s], a1_rsem.at[0, ys], sibling).wait_recv()
    for s in range(1, 4):
        rcopy(
            w0.at[x], w0.at[x], a2_ssem.at[0, s], a2_rsem.at[0, x], dev((x + s) % NX, y, z, c)
        ).start()
    for s in range(1, 4):
        xs = (x + s) % NX
        rcopy(w1.at[y, xs], w1.at[y, xs], a1_ssem.at[1, s], a1_rsem.at[1, xs], sibling).wait_recv()
    for s in range(1, 4):
        rcopy(
            w1.at[y], w1.at[y], a2_ssem.at[1, s], a2_rsem.at[1, y], dev(x, (y + s) % NY, z, c)
        ).start()

    pl.loop(PAIRS // 2, PAIRS)(forward)

    half = pl.ds(5 * c, 5)
    other = pl.ds(5 * (1 - c), 5)
    att_copy = rcopy(att.at[other], att_all.at[c], sib_ssem.at[0], sib_rsem.at[0], sibling)
    att_copy.start()
    att_all[c] = att[half]

    @pl.loop(1, NF)
    def _(s):
        frm = (f + s) % NF
        rcopy(dsend, drecv.at[frm], d_ssem.at[s], d_rsem.at[frm], sibling).wait_recv()

    dests = jnp.concatenate([drecv[k][0:1] for k in range(NF)], axis=0).astype(F32)
    owners = fdiv(dests, OWN)
    here = owners == f.astype(F32)
    before = jnp.where(row_i < col_i, 1.0, 0.0).astype(BF16)
    ranks = dot_nn(jnp.where(here, 1.0, 0.0).astype(BF16), before)
    ranks = jnp.where(here, ranks, -1.0).astype(BF16)
    slots = (dests - owners * OWN).astype(BF16)
    source = jnp.where(p_owner == iota((NF * 4 * CAP, NF), 1), 1.0, 0.0).astype(BF16)
    slot_col = jnp.sum(
        jnp.where(dot_nn(source, ranks) == p_rank, dot_nn(source, slots) + 1.0, 0.0),
        axis=1, keepdims=True,
    )
    slot_lane = iota((NF * 4 * CAP, OWN), 1) + 1.0

    @pl.loop(1, NF)
    def _(s):
        frm = (f + s) % NF
        rcopy(
            packed.at[frm], arrived.at[frm], c_ssem.at[s], c_rsem.at[frm], sibling
        ).wait_recv()

    rows_in = arrived[...].reshape(NF * 4 * CAP, QD)
    for k in range(4):
        place = jnp.where(
            jnp.where(p_quarter == k, slot_col, 0.0) == slot_lane, 1.0, 0.0
        ).astype(BF16)
        c_all[c, :, QD * k : QD * (k + 1)] = dot_tn(place, rows_in).astype(BF16)
    c_copy = rcopy(c_all.at[c], c_all.at[c], sib_ssem.at[1], sib_rsem.at[1], sibling)
    c_copy.start()
    rcopy(att.at[other], att_all.at[1 - c], sib_ssem.at[0], sib_rsem.at[0], sibling).wait_recv()
    att_t[...] = jnp.concatenate(
        [jnp.concatenate([att_all[g, i] for i in range(5)], axis=1) for g in range(2)], axis=0
    ).T
    rcopy(
        c_all.at[1 - c], c_all.at[1 - c], sib_ssem.at[1], sib_rsem.at[1], sibling
    ).wait_recv()

    for s in (1, 2, 3, 0):
        xs = (x + s) % NX
        cols = c_all[:, :, pl.ds(pl.multiple_of(xs * QD, 128), QD)].reshape(2 * OWN, QD)
        share = dot_nn(att_t[...], cols)
        for ys in range(NY):
            n = row_of(ys, 0)
            s0[xs, ys] = share[ROWS * n : ROWS * (n + 1)].astype(BF16)
            n = row_of(ys, 1)
            s1[ys, xs] = share[ROWS * n : ROWS * (n + 1)].astype(BF16)
        if s:
            rcopy(
                s0.at[xs], r0.at[x], b2_ssem.at[0, s], b2_rsem.at[0, x], dev(xs, y, z, c)
            ).start()
    for s in range(1, 4):
        ys = (y + s) % NY
        rcopy(
            s1.at[ys], r1.at[y], b2_ssem.at[1, s], b2_rsem.at[1, y], dev(x, ys, z, c)
        ).start()

    for s in range(1, 4):
        xs, ys = (x + s) % NX, (y + s) % NY
        rcopy(w0.at[xs], w0.at[xs], a2_ssem.at[0, s], a2_rsem.at[0, xs], sibling).wait_recv()
        rcopy(w1.at[ys], w1.at[ys], a2_ssem.at[1, s], a2_rsem.at[1, ys], sibling).wait_recv()
    total = None
    for k in range(4):
        blocks = []
        for n in range(8):
            ys, j = 2 * (n // 4) + n % 2, (n // 2) % 2
            blocks.append(w0[k, ys] if j == 0 else w1[ys, k])
        wk = jnp.concatenate(blocks, axis=0)
        cols = c_all[:, :, QD * k : QD * (k + 1)].reshape(2 * OWN, QD)
        term = dot_nt(cols, wk)
        total = term if total is None else total + term
    total = total.astype(BF16)
    for g in range(2):
        for i in range(5):
            g_tmp[g, i] = total[OWN * g : OWN * (g + 1), 128 * i : 128 * (i + 1)]
    g_copy = rcopy(g_tmp.at[1 - c], g_v.at[half], sib_ssem.at[2], sib_rsem.at[2], sibling)
    g_copy.start()
    g_v[half] = g_tmp[c]

    live = ids_col >= 0.0

    def backward(p):
        at = pl.ds(pl.multiple_of(p * 128, 128), 128)
        qp, kp, vp = q_v[:, at], k_v[:, at], v_v[:, at]
        gp = g_v[p]
        dqs, dks, dvs = [], [], []
        for i in range(2):
            prob = probs[2 * p + i]
            dvs.append(dot_tn(prob.astype(BF16), gp))
            pg = dot_nt(gp * head_masks[i], vp)
            delta = jnp.sum(prob * pg, axis=1, keepdims=True)
            sg = (prob * (pg - delta)).astype(BF16)
            dqs.append(dot_nn(sg, kp))
            dks.append(dot_tn(sg, qp))

        def put(ref, parts, scale):
            value = jnp.where(first_head, parts[0], parts[1]) * scale
            ref[:, at] = jnp.where(live, value, 0.0).astype(BF16)

        put(dq_v, dqs, SCALE)
        put(dk_v, dks, SCALE)
        put(dv_v, dvs, 1.0)

    mine_first = 5 * c
    pl.loop(0, PAIRS // 2)(lambda i: backward(mine_first + i))
    rcopy(
        g_tmp.at[1 - c], g_v.at[other], sib_ssem.at[2], sib_rsem.at[2], sibling
    ).wait_recv()
    theirs_first = 5 * (1 - c)
    pl.loop(0, PAIRS // 2)(lambda i: backward(theirs_first + i))
    outs = [
        pltpu.make_async_copy(src, dst, out_sem.at[i])
        for i, (src, dst) in enumerate(((dq_v, dq_hbm), (dk_v, dk_hbm), (dv_v, dv_hbm)))
    ]
    for out in outs:
        out.start()

    for s in range(1, 4):
        xs = (x + s) % NX
        rcopy(s0.at[xs], r0.at[xs], b2_ssem.at[0, s], b2_rsem.at[0, xs], sibling).wait_recv()
    for s in (1, 2, 3, 0):
        ys = (y + s) % NY
        acc = s0[x, ys].astype(F32)
        for e in range(1, 4):
            acc += r0[(x + e) % NX, ys].astype(F32)
        t0[ys] = acc.astype(BF16)
        if s:
            rcopy(
                t0.at[ys], u0.at[y], b1_ssem.at[0, s], b1_rsem.at[0, y], dev(x, ys, z, c)
            ).start()
        else:
            vf[0] = acc
    for s in range(1, 4):
        ys = (y + s) % NY
        rcopy(s1.at[ys], r1.at[ys], b2_ssem.at[1, s], b2_rsem.at[1, ys], sibling).wait_recv()
    for s in (1, 2, 3, 0):
        xs = (x + s) % NX
        acc = s1[y, xs].astype(F32)
        for e in range(1, 4):
            acc += r1[(y + e) % NY, xs].astype(F32)
        t1[xs] = acc.astype(BF16)
        if s:
            rcopy(
                t1.at[xs], u1.at[x], b1_ssem.at[1, s], b1_rsem.at[1, x], dev(xs, y, z, c)
            ).start()
        else:
            vf[1] = acc

    for j, (me, src, dst) in enumerate(((y, t0, u0), (x, t1, u1))):
        acc = vf[j]
        for s in range(1, 4):
            frm = (me + s) % 4
            rcopy(
                src.at[frm], dst.at[frm], b1_ssem.at[j, s], b1_rsem.at[j, frm], sibling
            ).wait_recv()
            acc += dst[frm].astype(F32)
        vf[j] = acc
        vb[j] = acc.astype(BF16)
        z_root = 4 * c + 2 * h + j

        @pl.when(z != z_root)
        def _(j=j, z_root=z_root):
            rcopy(
                vb.at[j], zr.at[z], bz_ssem.at[j], bz_rsem.at[z], dev(x, y, z_root, c)
            ).start()

    def emit(i):
        pltpu.make_async_copy(
            fall.at[i],
            wg_hbm.at[:, pl.ds(pl.multiple_of(i * QD, 128), QD)],
            wg_sem.at[i],
        ).start()

    y_twin = (y + 2) % NY

    @pl.when(root)
    def _():
        acc = vf[z % 2]
        for s in range(1, NZ):
            frm = (z + s) % NZ
            rcopy(vb.at[0], zr.at[frm], bz_ssem.at[0], bz_rsem.at[frm], sibling).wait_recv()
            acc += zr[frm].astype(F32)
        fall[x] = acc
        rcopy(fall.at[x], fall.at[x], f1_ssem, f1_rsem, dev(x, y_twin, z, c)).start()

    @pl.when(jnp.logical_and(active, (z % 4) // 2 != h))
    def _():
        rcopy(fall.at[x], fall.at[x], f1_ssem, f1_rsem, sibling).wait_recv()

    @pl.when(active)
    def _():
        for s in range(1, 4):
            rcopy(
                fall.at[x], fall.at[x], f2_ssem.at[s], f2_rsem.at[x], dev((x + s) % NX, y, z, c)
            ).start()
        for s in range(4):
            xs = (x + s) % NX
            if s:
                rcopy(
                    fall.at[xs], fall.at[xs], f2_ssem.at[s], f2_rsem.at[xs], sibling
                ).wait_recv()
            rcopy(fall.at[xs], fall.at[xs], f3_ssem.at[xs], f3_rsem.at[xs], sibling).start()
            emit(xs)

    @pl.when(jnp.logical_not(active))
    def _():
        for s in range(4):
            xs = (x + s) % NX
            rcopy(
                fall.at[xs], fall.at[xs], f3_ssem.at[xs], f3_rsem.at[xs], sibling
            ).wait_recv()
            emit(xs)

    @pl.when(root)
    def _():
        @pl.loop(1, NZ)
        def _(s):
            rcopy(w_mine, w0_mine, az_ssem.at[s], az_rsem.at[0], sibling).wait_send()

        rcopy(fall.at[x], fall.at[x], f1_ssem, f1_rsem, sibling).wait_send()

    @pl.loop(1, NF)
    def _(s):
        rcopy(dsend, drecv.at[f], d_ssem.at[s], d_rsem.at[f], sibling).wait_send()
        rcopy(packed.at[f], arrived.at[f], c_ssem.at[s], c_rsem.at[f], sibling).wait_send()

    for s in range(1, 4):
        for j, w in enumerate((w0_mine, w1_mine)):
            rcopy(w, w, a1_ssem.at[j, s], a1_rsem.at[j, 0], sibling).wait_send()
        for j, w in enumerate((w0.at[x], w1.at[y])):
            rcopy(w, w, a2_ssem.at[j, s], a2_rsem.at[j, 0], sibling).wait_send()
        for j, w in enumerate((s0.at[x], s1.at[y])):
            rcopy(w, w, b2_ssem.at[j, s], b2_rsem.at[j, 0], sibling).wait_send()
        for j, w in enumerate((t0.at[y], t1.at[x])):
            rcopy(w, w, b1_ssem.at[j, s], b1_rsem.at[j, 0], sibling).wait_send()
    att_copy.wait_send()
    c_copy.wait_send()
    g_copy.wait_send()
    for j in range(2):

        @pl.when(z != 4 * c + 2 * h + j)
        def _(j=j):
            rcopy(vb.at[j], zr.at[z], bz_ssem.at[j], bz_rsem.at[z], sibling).wait_send()

    @pl.when(active)
    def _():
        for s in range(1, 4):
            rcopy(fall.at[x], fall.at[x], f2_ssem.at[s], f2_rsem.at[x], sibling).wait_send()
        for s in range(4):
            rcopy(fall.at[s], fall.at[s], f3_ssem.at[s], f3_rsem.at[s], sibling).wait_send()

    for out in outs:
        out.wait()
    for i in range(4):
        pltpu.make_async_copy(
            fall.at[i], wg_hbm.at[:, QD * i : QD * (i + 1)], wg_sem.at[i]
        ).wait()


def per_device(cotangent, out_weight, queries, key_vectors, value_vectors, destination, protein_ids):
    dma = pltpu.SemaphoreType.DMA
    vmem = pltpu.VMEM
    slots = jax.ShapeDtypeStruct((OWN, PAIRS * 128), BF16)
    any_space = pl.BlockSpec(memory_space=pl.ANY)
    in_vmem = pl.BlockSpec(memory_space=pltpu.VMEM)
    return pl.pallas_call(
        kernel,
        out_shape=(slots, slots, slots, jax.ShapeDtypeStruct((ROWS, D), F32)),
        in_specs=[any_space] * 5 + [in_vmem] * 2,
        out_specs=(any_space,) * 4,
        scratch_shapes=[
            vmem((TOK, D), BF16),
            *[vmem((OWN, PAIRS * 128), BF16) for _ in range(6)],
            vmem((8, TOK), jnp.int32),
            vmem((NF, 8, TOK), jnp.int32),
            vmem((NF, 4 * CAP, QD), BF16),
            vmem((NF, 4 * CAP, QD), BF16),
            vmem((2, OWN, D), BF16),
            vmem((PAIRS, OWN, 128), BF16),
            vmem((2, 5, OWN, 128), BF16),
            vmem((640, 2 * OWN), BF16),
            vmem((2 * PAIRS, OWN, OWN), F32),
            vmem((OWN, OWN), F32),
            vmem((NX, NY, ROWS, QD), BF16),
            vmem((NY, NX, ROWS, QD), BF16),
            vmem((2, 5, OWN, 128), BF16),
            vmem((PAIRS, OWN, 128), BF16),
            *[vmem((4, 4, ROWS, QD), BF16) for _ in range(4)],
            *[vmem((4, ROWS, QD), BF16) for _ in range(4)],
            vmem((2, ROWS, QD), F32),
            vmem((2, ROWS, QD), BF16),
            vmem((NZ, ROWS, QD), BF16),
            vmem((NX, ROWS, QD), F32),
            dma((4,)), dma((3,)), dma((4,)), dma,
            dma((NF,)), dma((NF,)), dma((NF,)), dma((NF,)),
            dma((NZ,)), dma((2,)), dma((2, 4)), dma((2, 4)), dma((2, 4)), dma((2, 4)),
            dma((3,)), dma((3,)),
            dma((2, 4)), dma((2, 4)), dma((2, 4)), dma((2, 4)), dma((2,)), dma((NZ,)),
            dma, dma, dma((4,)), dma((4,)), dma((4,)), dma((4,)),
        ],
        compiler_params=pltpu.CompilerParams(
            collective_id=0, has_side_effects=True, vmem_limit_bytes=56 * 1024 * 1024
        ),
    )(
        cotangent, out_weight, queries, key_vectors, value_vectors,
        destination.reshape(1, TOK), protein_ids.reshape(1, OWN),
    )


def solution(mesh):
    rows = P(("dp", "fsdp"), None)
    return jax.shard_map(
        per_device,
        mesh=mesh,
        in_specs=(rows, P("fsdp", None), rows, rows, rows, P(("dp", "fsdp")), P(("dp", "fsdp"))),
        out_specs=(rows, rows, rows, P("fsdp", None)),
        check_vma=False,
    )
```

```python
import jax
import jax.numpy as jnp
from jax import lax
from jax.experimental import pallas as pl
from jax.experimental.pallas import tpu as pltpu
from jax.sharding import PartitionSpec as P

F32 = jnp.float32
BF16 = jnp.bfloat16
MESH = pl.DeviceIdType.MESH

NX, NY, NZ, NF = 4, 4, 8, 16
TOK = 128
OWN = 192
CAP = 12
D = 2560
QD = D // 4
ROWS = 80
BLK = 64
SPAD = 256
PAIRS = 10
SCALE = 0.125


def fdiv(values, by):
    return jnp.floor((values + 0.5) * (1.0 / by))


def iota(shape, dim):
    return lax.broadcasted_iota(jnp.int32, shape, dim).astype(F32)


def dot_nt(a, b):
    return lax.dot_general(a, b, (((1,), (1,)), ((), ())), preferred_element_type=F32)


def dot_tn(a, b):
    return lax.dot_general(a, b, (((0,), (0,)), ((), ())), preferred_element_type=F32)


def dot_nn(a, b):
    return jnp.dot(a, b, preferred_element_type=F32)


def row_of(y, j):
    return 4 * j + y


def kernel(
    cot_hbm, w_hbm, q_hbm, k_hbm, v_hbm, dest_ref, ids_ref,
    dq_hbm, dk_hbm, dv_hbm, wg_hbm,
    q_v, k_v, v_v, dq_v, dk_v, dv_v,
    dsend, drecv, c_all, h_own, h_tok,
    att, att_out, att_in, att_t, att_all, probs, same_v,
    w0, w1, g_tmp, g_tok, g_out, g_in, g_v,
    s0, s1, r0, r1, t0, t1, u0, u1, vf, vb, zr, fall,
    load_sem, out_sem, wg_sem, own_sem,
    d_ssem, d_rsem, c_ssem, c_rsem, g_ssem, g_rsem,
    az_ssem, az_rsem, a1_ssem, a1_rsem, a2_ssem, a2_rsem,
    sib_ssem, sib_rsem,
    b2_ssem, b2_rsem, b1_ssem, b1_rsem, bz_ssem, bz_rsem,
    f2_ssem, f2_rsem, f3_ssem, f3_rsem,
):
    dp = lax.axis_index("dp")
    f = lax.axis_index("fsdp")
    c = dp % 2
    x = (dp // 2) % NX
    h = dp // 8
    z = f // 2
    y = 2 * h + f % 2
    o = 1 - c

    def dev(x_, y_, z_, c_):
        return (((y_ // 2) * NX + x_) * 2 + c_, z_ * 2 + y_ % 2)

    def rcopy(src, dst, ssem, rsem, target):
        return pltpu.make_async_remote_copy(
            src_ref=src, dst_ref=dst, send_sem=ssem, recv_sem=rsem,
            device_id=target, device_id_type=MESH,
        )

    sibling = dev(x, y, z, o)

    loads = [
        pltpu.make_async_copy(src, dst, load_sem.at[i])
        for i, (src, dst) in enumerate(
            ((q_hbm, q_v), (k_hbm, k_v), (v_hbm, v_v), (cot_hbm, c_all.at[c]))
        )
    ]
    for load in loads:
        load.start()

    barrier = pltpu.get_barrier_semaphore()

    @pl.loop(1, NF)
    def _(s):
        pl.semaphore_signal(
            barrier, inc=1, device_id=(dp, (f + s) % NF), device_id_type=MESH
        )

    for s in range(1, 4):
        pl.semaphore_signal(
            barrier, inc=1, device_id=dev((x + s) % NX, y, z, c), device_id_type=MESH
        )
        pl.semaphore_signal(
            barrier, inc=1, device_id=dev(x, (y + s) % NY, z, c), device_id_type=MESH
        )
        pl.semaphore_signal(
            barrier, inc=1, device_id=dev((x + s) % NX, (y + 2) % NY, z, c), device_id_type=MESH
        )
    pl.semaphore_signal(barrier, inc=1, device_id=sibling, device_id_type=MESH)

    ids = ids_ref[...].astype(F32)
    srow = iota((OWN, OWN), 0)
    scol = iota((OWN, OWN), 1)
    ids_col = jnp.sum(
        jnp.where(srow == scol, jnp.broadcast_to(ids, (OWN, OWN)), 0.0), axis=1, keepdims=True
    )
    same_v[...] = jnp.where(ids_col == ids, 1.0, 0.0)
    dest = dest_ref[...]
    dsend[...] = jnp.broadcast_to(dest, (8, TOK))
    att[:, OWN:SPAD] = jnp.zeros((PAIRS, SPAD - OWN, 128), BF16)
    lane = lax.broadcasted_iota(jnp.int32, (1, 128), 1)
    head_masks = (
        jnp.where(lane < 64, 1.0, 0.0).astype(BF16),
        jnp.where(lane < 64, 0.0, 1.0).astype(BF16),
    )
    first_head = lax.broadcasted_iota(jnp.int32, (OWN, 128), 1) < 64

    pl.semaphore_wait(barrier, 25)

    @pl.loop(1, NF)
    def _(s):
        rcopy(dsend, drecv.at[f], d_ssem.at[s], d_rsem.at[f], (dp, (f + s) % NF)).start()

    drecv[f] = dsend[...]

    active = z // 4 == c
    root = jnp.logical_and(active, z % 2 == h)
    root_j = (z % 4) // 2
    w_mine = w_hbm.at[:, pl.ds(pl.multiple_of(x * QD, 128), QD)]

    def spread_z(dst):
        pltpu.make_async_copy(w_mine, dst, own_sem).start()

        @pl.loop(1, NZ)
        def _(s):
            rcopy(
                w_mine, dst, az_ssem.at[s], az_rsem.at[root_j], dev(x, y, (z + s) % NZ, c)
            ).start()

    w0_mine = w0.at[x, y]
    w1_mine = w1.at[y, x]

    @pl.when(jnp.logical_and(root, root_j == 0))
    def _():
        spread_z(w0_mine)

    @pl.when(jnp.logical_and(root, root_j == 1))
    def _():
        spread_z(w1_mine)

    c_copy = rcopy(cot_hbm, c_all.at[c], sib_ssem.at[1], sib_rsem.at[1], sibling)
    c_copy.start()

    def both_heads(rows):
        return jnp.concatenate([rows * head_masks[0], rows * head_masks[1]], axis=0)

    def forward(p):
        at = pl.ds(pl.multiple_of(p * 128, 128), 128)
        qp, kp, vp = q_v[:, at], k_v[:, at], v_v[:, at]
        scores = dot_nt(both_heads(qp), kp) * SCALE
        same = jnp.concatenate([same_v[...], same_v[...]], axis=0)
        scores = jnp.where(same > 0.0, scores, -1e30)
        top = jnp.max(scores, axis=1, keepdims=True)
        e = jnp.exp(scores - top)
        prob = e * (1.0 / jnp.sum(e, axis=1, keepdims=True))
        probs[p] = prob
        out = dot_nn(prob.astype(BF16), vp)
        att[p, 0:OWN] = jnp.where(first_head, out[:OWN], out[OWN:]).astype(BF16)

    for load in loads[:3]:
        load.wait()
    pl.loop(0, 5)(lambda i: forward(5 * o + i))

    @pl.loop(1, NF)
    def _(s):
        frm = (f + s) % NF
        rcopy(dsend, drecv.at[frm], d_ssem.at[s], d_rsem.at[frm], sibling).wait_recv()

    row_i = iota((TOK, TOK), 0)
    col_i = iota((TOK, TOK), 1)
    p_col = iota((NF * BLK, 1), 0)
    p_dev = fdiv(p_col, BLK)
    p_in = p_col - p_dev * BLK
    p_pair = fdiv(p_in, CAP)
    p_rank = p_in - p_pair * CAP
    dests = jnp.concatenate([drecv[k][0:1] for k in range(NF)], axis=0).astype(F32)
    owners = fdiv(dests, OWN)
    here = owners == f.astype(F32)
    before = jnp.where(row_i < col_i, 1.0, 0.0).astype(BF16)
    ranks = dot_nn(jnp.where(here, 1.0, 0.0).astype(BF16), before)
    ranks = jnp.where(here, ranks, -1.0).astype(BF16)
    slots = (dests - owners * OWN).astype(BF16)
    source = jnp.where(p_dev == iota((NF * BLK, NF), 1), 1.0, 0.0).astype(BF16)
    slot_col = jnp.sum(
        jnp.where(dot_nn(source, ranks) == p_rank, dot_nn(source, slots) + 1.0, 0.0),
        axis=1, keepdims=True,
    )
    slot_lane = iota((1, SPAD), 1) + 1.0
    for k in range(5):
        h_own[:, SPAD * k : SPAD * (k + 1)] = jnp.where(
            jnp.where(p_pair == k, slot_col, 0.0) == slot_lane, 1.0, 0.0
        ).astype(BF16)

    def send_att(n, part):
        rows = att[pl.ds(5 * part, 5)].reshape(5 * SPAD, 128)
        att_out[n] = dot_nn(h_own[...], rows).astype(BF16).reshape(NF, BLK, 128)

        @pl.loop(1, NF)
        def _(s):
            to = (f + s) % NF
            rcopy(
                att_out.at[n, to], att_in.at[n, f], c_ssem.at[n, s], c_rsem.at[n, f], (dp, to)
            ).start()

        att_in[n, f] = att_out[n, f]

    send_att(0, o)

    pl.loop(0, 2)(lambda i: forward(5 * c + i))

    def pass_on(j, k):
        for s in (1, 3, 2):
            ref = w0.at[x, k] if j == 0 else w1.at[y, k]
            to = dev((x + s) % NX, y, z, c) if j == 0 else dev(x, (y + s) % NY, z, c)
            me = x if j == 0 else y
            rcopy(ref, ref, a2_ssem.at[j, s, k], a2_rsem.at[j, me, k], to).start()

    @pl.when(root)
    def _():
        pltpu.make_async_copy(w_mine, w0_mine, own_sem).wait()

    @pl.when(z != 4 * c + h)
    def _():
        rcopy(w0_mine, w0_mine, az_ssem.at[0], az_rsem.at[0], sibling).wait_recv()

    for s in (1, 3, 2):
        rcopy(
            w0_mine, w0_mine, a1_ssem.at[0, s], a1_rsem.at[0, y], dev(x, (y + s) % NY, z, c)
        ).start()
    pass_on(0, y)

    @pl.when(z != 4 * c + 2 + h)
    def _():
        rcopy(w1_mine, w1_mine, az_ssem.at[0], az_rsem.at[1], sibling).wait_recv()

    for s in (1, 3, 2):
        rcopy(
            w1_mine, w1_mine, a1_ssem.at[1, s], a1_rsem.at[1, x], dev((x + s) % NX, y, z, c)
        ).start()
    pass_on(1, x)

    pl.loop(2, 5)(lambda i: forward(5 * c + i))
    send_att(1, c)

    dest_f = dest.astype(F32)
    owner = fdiv(dest_f, OWN)
    owner_col = jnp.sum(
        jnp.where(row_i == col_i, jnp.broadcast_to(owner, (TOK, TOK)), 0.0),
        axis=1, keepdims=True,
    )
    ahead = jnp.where(jnp.logical_and(owner_col == owner, row_i < col_i), 1.0, 0.0)
    position = owner * CAP + jnp.sum(ahead, axis=0, keepdims=True)
    p_pos = p_dev * CAP + p_rank
    for k in range(5):
        h_tok[:, TOK * k : TOK * (k + 1)] = jnp.where(
            jnp.where(p_pair == k, p_pos, -1.0) == position, 1.0, 0.0
        ).astype(BF16)

    for s in (1, 3, 2):
        ys, xs = (y + s) % NY, (x + s) % NX
        rcopy(w0.at[x, ys], w0.at[x, ys], a1_ssem.at[0, s], a1_rsem.at[0, ys], sibling).wait_recv()
        pass_on(0, ys)
        rcopy(w1.at[y, xs], w1.at[y, xs], a1_ssem.at[1, s], a1_rsem.at[1, xs], sibling).wait_recv()
        pass_on(1, xs)

    def take_att(n):
        @pl.loop(1, NF)
        def _(s):
            frm = (f + s) % NF
            rcopy(
                att_out.at[n, frm], att_in.at[n, frm], c_ssem.at[n, s], c_rsem.at[n, frm], sibling
            ).wait_recv()

        out = dot_tn(att_in[n].reshape(NF * BLK, 128), h_tok[...]).astype(BF16)
        return jnp.concatenate([out[:, TOK * k : TOK * (k + 1)] for k in range(5)], axis=0)

    att_t[...] = take_att(0)
    att_copy = rcopy(att_t, att_all.at[c], sib_ssem.at[0], sib_rsem.at[0], sibling)
    att_copy.start()
    att_all[c] = take_att(1)
    loads[3].wait()
    rcopy(cot_hbm, c_all.at[o], sib_ssem.at[1], sib_rsem.at[1], sibling).wait_recv()
    rcopy(att_t, att_all.at[o], sib_ssem.at[0], sib_rsem.at[0], sibling).wait_recv()

    def share_out(j, to, k):
        if j == 0:
            src, dst, me, device = s0.at[to, k], r0.at[x, k], x, dev(to, y, z, c)
        else:
            src, dst, me, device = s1.at[to, k], r1.at[y, k], y, dev(x, to, z, c)
        rcopy(src, dst, b2_ssem.at[j, to, k], b2_rsem.at[j, me, k], device).start()

    att_both = jnp.concatenate([att_all[0], att_all[1]], axis=1)
    for s in (1, 2, 3, 0):
        xs = (x + s) % NX
        cols = c_all[:, :, pl.ds(pl.multiple_of(xs * QD, 128), QD)].reshape(2 * TOK, QD)
        share = dot_nn(att_both, cols)
        for ys in range(NY):
            n = row_of(ys, 0)
            s0[xs, ys] = share[ROWS * n : ROWS * (n + 1)].astype(BF16)
            n = row_of(ys, 1)
            s1[ys, xs] = share[ROWS * n : ROWS * (n + 1)].astype(BF16)
        if s:
            share_out(0, xs, (y + 1) % NY)
        for e in (1, 3, 2):
            share_out(1, (y + e) % NY, xs)
    for e in (2, 3, 0):
        for s in (1, 3, 2):
            share_out(0, (x + s) % NX, (y + e) % NY)

    for s in range(1, 4):
        xs, ys = (x + s) % NX, (y + s) % NY
        for k in range(4):
            for j, ref, frm in ((0, w0.at[xs, k], xs), (1, w1.at[ys, k], ys)):
                rcopy(ref, ref, a2_ssem.at[j, s, k], a2_rsem.at[j, frm, k], sibling).wait_recv()
    total = None
    for k in range(4):
        blocks = []
        for n in range(8):
            ys, j = n % 4, n // 4
            blocks.append(w0[k, ys] if j == 0 else w1[ys, k])
        wk = jnp.concatenate(blocks, axis=0)
        cols = c_all[:, :, QD * k : QD * (k + 1)].reshape(2 * TOK, QD)
        term = dot_nt(cols, wk)
        total = term if total is None else total + term
    total = total.astype(BF16)
    for g in range(2):
        for i in range(5):
            g_tmp[g, i] = total[TOK * g : TOK * (g + 1), 128 * i : 128 * (i + 1)]
    g_copy = rcopy(g_tmp.at[o], g_tok, sib_ssem.at[2], sib_rsem.at[2], sibling)
    g_copy.start()

    def send_grad(n, rows):
        g_out[n] = dot_nn(h_tok[...], rows.reshape(5 * TOK, 128)).astype(BF16).reshape(NF, BLK, 128)

        @pl.loop(1, NF)
        def _(s):
            to = (f + s) % NF
            rcopy(
                g_out.at[n, to], g_in.at[n, f], g_ssem.at[n, s], g_rsem.at[n, f], (dp, to)
            ).start()

        g_in[n, f] = g_out[n, f]

    send_grad(0, g_tmp[c])
    rcopy(g_tmp.at[o], g_tok, sib_ssem.at[2], sib_rsem.at[2], sibling).wait_recv()
    send_grad(1, g_tok[...])

    for e in (1, 2, 3, 0):
        for j in range(2):
            if j == 0:
                own, ins, out, nxt, me, k = s0, r0, t0, u0, x, (y + e) % NY
                after, to = y, dev(x, k, z, c)
            else:
                own, ins, out, nxt, me, k = s1, r1, t1, u1, y, (x + e) % NX
                after, to = x, dev(k, y, z, c)
            acc = own[me, k].astype(F32)
            for s in (1, 3, 2):
                frm = (me + s) % 4
                rcopy(
                    own.at[frm, k], ins.at[frm, k], b2_ssem.at[j, 0, 0], b2_rsem.at[j, frm, k],
                    sibling,
                ).wait_recv()
                acc += ins[frm, k].astype(F32)
            if e:
                out[k] = acc.astype(BF16)
                rcopy(
                    out.at[k], nxt.at[after], b1_ssem.at[j, e], b1_rsem.at[j, after], to
                ).start()
            else:
                vf[j] = acc

    for j, (me, src, dst) in enumerate(((y, t0, u0), (x, t1, u1))):
        acc = vf[j]
        for s in range(1, 4):
            frm = (me + s) % 4
            rcopy(
                src.at[frm], dst.at[frm], b1_ssem.at[j, s], b1_rsem.at[j, frm], sibling
            ).wait_recv()
            acc += dst[frm].astype(F32)
        vf[j] = acc
        vb[j] = acc.astype(BF16)
        z_root = 4 * c + 2 * j + h

        @pl.when(z != z_root)
        def _(j=j, z_root=z_root):
            rcopy(
                vb.at[j], zr.at[z], bz_ssem.at[j], bz_rsem.at[z], dev(x, y, z_root, c)
            ).start()

    def take_grad(n):
        @pl.loop(1, NF)
        def _(s):
            frm = (f + s) % NF
            rcopy(
                g_out.at[n, frm], g_in.at[n, frm], g_ssem.at[n, s], g_rsem.at[n, frm], sibling
            ).wait_recv()

        out = dot_tn(g_in[n].reshape(NF * BLK, 128), h_own[...])
        for k in range(5):
            g_v[k] = out[:, SPAD * k : SPAD * (k + 1)].T[:OWN].astype(BF16)

    live = ids_col >= 0.0

    def backward(p, gp):
        at = pl.ds(pl.multiple_of(p * 128, 128), 128)
        qp, kp, vp = q_v[:, at], k_v[:, at], v_v[:, at]
        prob = probs[p]
        pg = dot_nt(both_heads(gp), vp)
        delta = jnp.sum(prob * pg, axis=1, keepdims=True)
        sg = (prob * (pg - delta)).astype(BF16)
        pb = prob.astype(BF16)
        dq = dot_nn(sg, kp)

        def put(ref, one, two, scale):
            value = jnp.where(first_head, one, two) * scale
            ref[:, at] = jnp.where(live, value, 0.0).astype(BF16)

        put(dq_v, dq[:OWN], dq[OWN:], SCALE)
        put(dk_v, dot_tn(sg[:OWN], qp), dot_tn(sg[OWN:], qp), SCALE)
        put(dv_v, dot_tn(pb[:OWN], gp), dot_tn(pb[OWN:], gp), 1.0)

    take_grad(0)
    pl.loop(0, 5)(lambda i: backward(5 * c + i, g_v[i]))
    take_grad(1)
    pl.loop(0, 5)(lambda i: backward(5 * o + i, g_v[i]))
    outs = [
        pltpu.make_async_copy(src, dst, out_sem.at[i])
        for i, (src, dst) in enumerate(((dq_v, dq_hbm), (dk_v, dk_hbm), (dv_v, dv_hbm)))
    ]
    for out in outs:
        out.start()

    def emit(i):
        pltpu.make_async_copy(
            fall.at[i],
            wg_hbm.at[:, pl.ds(pl.multiple_of(i * QD, 128), QD)],
            wg_sem.at[i],
        ).start()

    def to_sibling(i):
        rcopy(fall.at[i], fall.at[i], f3_ssem.at[i], f3_rsem.at[i], sibling).start()
        emit(i)

    @pl.when(root)
    def _():
        acc = vf[root_j]
        for s in range(1, NZ):
            frm = (z + s) % NZ
            rcopy(vb.at[0], zr.at[frm], bz_ssem.at[0], bz_rsem.at[frm], sibling).wait_recv()
            acc += zr[frm].astype(F32)
        fall[x] = acc.astype(BF16)
        for s in (1, 3, 2, 0):
            for e in (2, 0):
                if s or e:
                    rcopy(
                        fall.at[x], fall.at[x], f2_ssem.at[s, e // 2], f2_rsem.at[x],
                        dev((x + s) % NX, (y + e) % NY, z, c),
                    ).start()
        to_sibling(x)

    @pl.when(jnp.logical_and(active, z % 2 != h))
    def _():
        rcopy(fall.at[x], fall.at[x], f2_ssem.at[0, 0], f2_rsem.at[x], sibling).wait_recv()
        to_sibling(x)

    @pl.when(active)
    def _():
        for s in (1, 3, 2):
            xs = (x + s) % NX
            rcopy(fall.at[xs], fall.at[xs], f2_ssem.at[0, 0], f2_rsem.at[xs], sibling).wait_recv()
            to_sibling(xs)

    @pl.when(jnp.logical_not(active))
    def _():
        for s in (0, 1, 3, 2):
            xs = (x + s) % NX
            rcopy(
                fall.at[xs], fall.at[xs], f3_ssem.at[xs], f3_rsem.at[xs], sibling
            ).wait_recv()
            emit(xs)

    @pl.when(root)
    def _():
        @pl.loop(1, NZ)
        def _(s):
            rcopy(w_mine, w0_mine, az_ssem.at[s], az_rsem.at[0], sibling).wait_send()

        for s in range(4):
            for e in range(2):
                if s or e:
                    rcopy(
                        fall.at[x], fall.at[x], f2_ssem.at[s, e], f2_rsem.at[x], sibling
                    ).wait_send()

    @pl.loop(1, NF)
    def _(s):
        rcopy(dsend, drecv.at[f], d_ssem.at[s], d_rsem.at[f], sibling).wait_send()
        for n in range(2):
            rcopy(
                att_out.at[n, f], att_in.at[n, f], c_ssem.at[n, s], c_rsem.at[n, f], sibling
            ).wait_send()
            rcopy(
                g_out.at[n, f], g_in.at[n, f], g_ssem.at[n, s], g_rsem.at[n, f], sibling
            ).wait_send()

    for s in range(1, 4):
        for j, w in enumerate((w0_mine, w1_mine)):
            rcopy(w, w, a1_ssem.at[j, s], a1_rsem.at[j, 0], sibling).wait_send()
        for k in range(4):
            for j in range(2):
                rcopy(
                    w0_mine, w0_mine, a2_ssem.at[j, s, k], a2_rsem.at[j, 0, 0], sibling
                ).wait_send()
                to = ((x if j == 0 else y) + s) % 4
                rcopy(
                    w0_mine, w0_mine, b2_ssem.at[j, to, k], b2_rsem.at[j, 0, 0], sibling
                ).wait_send()
        for j, w in enumerate((t0.at[y], t1.at[x])):
            rcopy(w, w, b1_ssem.at[j, s], b1_rsem.at[j, 0], sibling).wait_send()
    att_copy.wait_send()
    c_copy.wait_send()
    g_copy.wait_send()
    for j in range(2):

        @pl.when(z != 4 * c + 2 * j + h)
        def _(j=j):
            rcopy(vb.at[j], zr.at[z], bz_ssem.at[j], bz_rsem.at[z], sibling).wait_send()

    @pl.when(active)
    def _():
        for s in range(4):
            rcopy(fall.at[s], fall.at[s], f3_ssem.at[s], f3_rsem.at[s], sibling).wait_send()

    for out in outs:
        out.wait()
    for i in range(4):
        pltpu.make_async_copy(
            fall.at[i], wg_hbm.at[:, QD * i : QD * (i + 1)], wg_sem.at[i]
        ).wait()


def finish(dq_in, dk_in, dv_in, wg_in, dq_out, dk_out, dv_out, wg_out, grads, wg_b, wg_f, sems):
    pairs = ((dq_in, dq_out), (dk_in, dk_out), (dv_in, dv_out))
    reads = [pltpu.make_async_copy(pairs[i][0], grads.at[i], sems.at[i]) for i in range(3)]
    reads.append(pltpu.make_async_copy(wg_in, wg_b, sems.at[3]))
    writes = [pltpu.make_async_copy(grads.at[i], pairs[i][1], sems.at[i]) for i in range(3)]
    writes.append(pltpu.make_async_copy(wg_f, wg_out, sems.at[3]))
    for read in reads:
        read.start()
    for i in range(3):
        reads[i].wait()
        writes[i].start()
    reads[3].wait()
    wg_f[...] = wg_b[...].astype(F32)
    for write in writes[3:]:
        write.start()
    for write in writes:
        write.wait()


def per_device(cotangent, out_weight, queries, key_vectors, value_vectors, destination, protein_ids):
    dma = pltpu.SemaphoreType.DMA
    vmem = pltpu.VMEM
    slots = jax.ShapeDtypeStruct((OWN, PAIRS * 128), BF16)
    any_space = pl.BlockSpec(memory_space=pl.ANY)
    in_vmem = pl.BlockSpec(memory_space=pltpu.VMEM)
    *grads, weight_grad = pl.pallas_call(
        kernel,
        out_shape=(slots, slots, slots, jax.ShapeDtypeStruct((ROWS, D), BF16)),
        in_specs=[any_space] * 5 + [in_vmem] * 2,
        out_specs=(any_space,) * 4,
        scratch_shapes=[
            *[vmem((OWN, PAIRS * 128), BF16) for _ in range(6)],
            vmem((8, TOK), jnp.int32),
            vmem((NF, 8, TOK), jnp.int32),
            vmem((2, TOK, D), BF16),
            vmem((NF * BLK, 5 * SPAD), BF16),
            vmem((NF * BLK, 5 * TOK), BF16),
            vmem((PAIRS, SPAD, 128), BF16),
            vmem((2, NF, BLK, 128), BF16),
            vmem((2, NF, BLK, 128), BF16),
            vmem((640, TOK), BF16),
            vmem((2, 640, TOK), BF16),
            vmem((PAIRS, 2 * OWN, OWN), F32),
            vmem((OWN, OWN), F32),
            vmem((NX, NY, ROWS, QD), BF16),
            vmem((NY, NX, ROWS, QD), BF16),
            vmem((2, 5, TOK, 128), BF16),
            vmem((5, TOK, 128), BF16),
            vmem((2, NF, BLK, 128), BF16),
            vmem((2, NF, BLK, 128), BF16),
            vmem((5, OWN, 128), BF16),
            *[vmem((4, 4, ROWS, QD), BF16) for _ in range(4)],
            *[vmem((4, ROWS, QD), BF16) for _ in range(4)],
            vmem((2, ROWS, QD), F32),
            vmem((2, ROWS, QD), BF16),
            vmem((NZ, ROWS, QD), BF16),
            vmem((NX, ROWS, QD), BF16),
            dma((4,)), dma((3,)), dma((4,)), dma,
            dma((NF,)), dma((NF,)), *[dma((2, NF)) for _ in range(4)],
            dma((NZ,)), dma((2,)), dma((2, 4)), dma((2, 4)), dma((2, 4, 4)), dma((2, 4, 4)),
            dma((3,)), dma((3,)),
            dma((2, 4, 4)), dma((2, 4, 4)), dma((2, 4)), dma((2, 4)), dma((2,)), dma((NZ,)),
            dma((4, 2)), dma((4,)), dma((4,)), dma((4,)),
        ],
        compiler_params=pltpu.CompilerParams(
            collective_id=0, has_side_effects=True, vmem_limit_bytes=56 * 1024 * 1024
        ),
    )(
        cotangent, out_weight, queries, key_vectors, value_vectors,
        destination.reshape(1, TOK), protein_ids.reshape(1, OWN),
    )
    return pl.pallas_call(
        finish,
        out_shape=(slots, slots, slots, jax.ShapeDtypeStruct((ROWS, D), F32)),
        in_specs=[any_space] * 4,
        out_specs=(any_space,) * 4,
        scratch_shapes=[vmem((3, OWN, PAIRS * 128), BF16), vmem((ROWS, D), BF16), vmem((ROWS, D), F32), dma((4,))],
    )(*grads, weight_grad)


def solution(mesh):
    rows = P(("dp", "fsdp"), None)
    return jax.shard_map(
        per_device,
        mesh=mesh,
        in_specs=(rows, P("fsdp", None), rows, rows, rows, P(("dp", "fsdp")), P(("dp", "fsdp"))),
        out_specs=(rows, rows, rows, P("fsdp", None)),
        check_vma=False,
    )
```

```python
import jax
import jax.numpy as jnp
from jax import lax
from jax.experimental import pallas as pl
from jax.experimental.pallas import tpu as pltpu
from jax.sharding import PartitionSpec as P

F32 = jnp.float32
BF16 = jnp.bfloat16
MESH = pl.DeviceIdType.MESH

NX, NY, NZ, NF = 4, 4, 8, 16
TOK = 128
OWN = 192
CAP = 12
D = 2560
QD = D // 4
ROWS = 80
BLK = 64
SPAD = 256
PAIRS = 10
SCALE = 0.125


def fdiv(values, by):
    return jnp.floor((values + 0.5) * (1.0 / by))


def iota(shape, dim):
    return lax.broadcasted_iota(jnp.int32, shape, dim).astype(F32)


def dot_nt(a, b):
    return lax.dot_general(a, b, (((1,), (1,)), ((), ())), preferred_element_type=F32)


def dot_tn(a, b):
    return lax.dot_general(a, b, (((0,), (0,)), ((), ())), preferred_element_type=F32)


def dot_nn(a, b):
    return jnp.dot(a, b, preferred_element_type=F32)


def row_of(y, j):
    return 4 * j + y


def kernel(
    cot_hbm, w_hbm, q_hbm, k_hbm, v_hbm, dest_ref, ids_ref,
    dq_hbm, dk_hbm, dv_hbm, wg_hbm,
    q_v, k_v, v_v, dq_v, dk_v, dv_v,
    dsend, drecv, c_all, h_own, h_tok,
    att, att_out, att_in, att_t, att_all, probs, same_v,
    w0, w1, g_tmp, g_tok, g_out, g_in, g_v,
    s0, s1, r0, r1, m_in, m_out, t0, t1, u0, u1, vf, vb, zr, fall,
    load_sem, out_sem, wg_sem, own_sem,
    d_ssem, d_rsem, c_ssem, c_rsem, g_ssem, g_rsem,
    az_ssem, az_rsem, a1_ssem, a1_rsem, a2_ssem, a2_rsem,
    sib_ssem, sib_rsem,
    m_ssem, m_rsem, b2_ssem, b2_rsem, b1_ssem, b1_rsem, bz_ssem, bz_rsem,
    f2_ssem, f2_rsem, f3_ssem, f3_rsem,
):
    dp = lax.axis_index("dp")
    f = lax.axis_index("fsdp")
    c = dp % 2
    x = (dp // 2) % NX
    h = dp // 8
    z = f // 2
    y = 2 * h + f % 2
    o = 1 - c

    def dev(x_, y_, z_, c_):
        return (((y_ // 2) * NX + x_) * 2 + c_, z_ * 2 + y_ % 2)

    def rcopy(src, dst, ssem, rsem, target):
        return pltpu.make_async_remote_copy(
            src_ref=src, dst_ref=dst, send_sem=ssem, recv_sem=rsem,
            device_id=target, device_id_type=MESH,
        )

    sibling = dev(x, y, z, o)

    loads = [
        pltpu.make_async_copy(src, dst, load_sem.at[i])
        for i, (src, dst) in enumerate(
            ((q_hbm, q_v), (k_hbm, k_v), (v_hbm, v_v), (cot_hbm, c_all.at[c]))
        )
    ]
    for load in loads:
        load.start()

    barrier = pltpu.get_barrier_semaphore()

    @pl.loop(1, NF)
    def _(s):
        pl.semaphore_signal(
            barrier, inc=1, device_id=(dp, (f + s) % NF), device_id_type=MESH
        )

    for s in range(1, 4):
        pl.semaphore_signal(
            barrier, inc=1, device_id=dev((x + s) % NX, y, z, c), device_id_type=MESH
        )
        pl.semaphore_signal(
            barrier, inc=1, device_id=dev(x, (y + s) % NY, z, c), device_id_type=MESH
        )
        pl.semaphore_signal(
            barrier, inc=1, device_id=dev((x + s) % NX, (y + 2) % NY, z, c), device_id_type=MESH
        )
    pl.semaphore_signal(barrier, inc=1, device_id=sibling, device_id_type=MESH)

    ids = ids_ref[...].astype(F32)
    srow = iota((OWN, OWN), 0)
    scol = iota((OWN, OWN), 1)
    ids_col = jnp.sum(
        jnp.where(srow == scol, jnp.broadcast_to(ids, (OWN, OWN)), 0.0), axis=1, keepdims=True
    )
    same_v[...] = jnp.where(ids_col == ids, 1.0, 0.0)
    dest = dest_ref[...]
    dsend[...] = jnp.broadcast_to(dest, (8, TOK))
    att[:, OWN:SPAD] = jnp.zeros((PAIRS, SPAD - OWN, 128), BF16)
    lane = lax.broadcasted_iota(jnp.int32, (1, 128), 1)
    head_masks = (
        jnp.where(lane < 64, 1.0, 0.0).astype(BF16),
        jnp.where(lane < 64, 0.0, 1.0).astype(BF16),
    )
    first_head = lax.broadcasted_iota(jnp.int32, (OWN, 128), 1) < 64

    pl.semaphore_wait(barrier, 25)

    @pl.loop(1, NF)
    def _(s):
        rcopy(dsend, drecv.at[f], d_ssem.at[s], d_rsem.at[f], (dp, (f + s) % NF)).start()

    drecv[f] = dsend[...]

    active = z // 4 == c
    root = jnp.logical_and(active, z % 2 == h)
    root_j = (z % 4) // 2
    w_mine = w_hbm.at[:, pl.ds(pl.multiple_of(x * QD, 128), QD)]

    def spread_z(dst):
        pltpu.make_async_copy(w_mine, dst, own_sem).start()

        @pl.loop(1, NZ)
        def _(s):
            rcopy(
                w_mine, dst, az_ssem.at[s], az_rsem.at[root_j], dev(x, y, (z + s) % NZ, c)
            ).start()

    w0_mine = w0.at[x, y]
    w1_mine = w1.at[y, x]

    @pl.when(jnp.logical_and(root, root_j == 0))
    def _():
        spread_z(w0_mine)

    @pl.when(jnp.logical_and(root, root_j == 1))
    def _():
        spread_z(w1_mine)

    c_copy = rcopy(cot_hbm, c_all.at[c], sib_ssem.at[1], sib_rsem.at[1], sibling)
    c_copy.start()

    def both_heads(rows):
        return jnp.concatenate([rows * head_masks[0], rows * head_masks[1]], axis=0)

    def forward(p):
        at = pl.ds(pl.multiple_of(p * 128, 128), 128)
        qp, kp, vp = q_v[:, at], k_v[:, at], v_v[:, at]
        scores = dot_nt(both_heads(qp), kp) * SCALE
        same = jnp.concatenate([same_v[...], same_v[...]], axis=0)
        scores = jnp.where(same > 0.0, scores, -1e30)
        top = jnp.max(scores, axis=1, keepdims=True)
        e = jnp.exp(scores - top)
        prob = e * (1.0 / jnp.sum(e, axis=1, keepdims=True))
        probs[p] = prob
        out = dot_nn(prob.astype(BF16), vp)
        att[p, 0:OWN] = jnp.where(first_head, out[:OWN], out[OWN:]).astype(BF16)

    for load in loads[:3]:
        load.wait()
    pl.loop(0, 5)(lambda i: forward(5 * o + i))

    @pl.loop(1, NF)
    def _(s):
        frm = (f + s) % NF
        rcopy(dsend, drecv.at[frm], d_ssem.at[s], d_rsem.at[frm], sibling).wait_recv()

    row_i = iota((TOK, TOK), 0)
    col_i = iota((TOK, TOK), 1)
    p_col = iota((NF * BLK, 1), 0)
    p_dev = fdiv(p_col, BLK)
    p_in = p_col - p_dev * BLK
    p_pair = fdiv(p_in, CAP)
    p_rank = p_in - p_pair * CAP
    dests = jnp.concatenate([drecv[k][0:1] for k in range(NF)], axis=0).astype(F32)
    owners = fdiv(dests, OWN)
    here = owners == f.astype(F32)
    before = jnp.where(row_i < col_i, 1.0, 0.0).astype(BF16)
    ranks = dot_nn(jnp.where(here, 1.0, 0.0).astype(BF16), before)
    ranks = jnp.where(here, ranks, -1.0).astype(BF16)
    slots = (dests - owners * OWN).astype(BF16)
    source = jnp.where(p_dev == iota((NF * BLK, NF), 1), 1.0, 0.0).astype(BF16)
    slot_col = jnp.sum(
        jnp.where(dot_nn(source, ranks) == p_rank, dot_nn(source, slots) + 1.0, 0.0),
        axis=1, keepdims=True,
    )
    slot_lane = iota((1, SPAD), 1) + 1.0
    for k in range(5):
        h_own[:, SPAD * k : SPAD * (k + 1)] = jnp.where(
            jnp.where(p_pair == k, slot_col, 0.0) == slot_lane, 1.0, 0.0
        ).astype(BF16)

    def send_att(n, part):
        rows = att[pl.ds(5 * part, 5)].reshape(5 * SPAD, 128)
        att_out[n] = dot_nn(h_own[...], rows).astype(BF16).reshape(NF, BLK, 128)

        @pl.loop(1, NF)
        def _(s):
            to = (f + s) % NF
            rcopy(
                att_out.at[n, to], att_in.at[n, f], c_ssem.at[n, s], c_rsem.at[n, f], (dp, to)
            ).start()

        att_in[n, f] = att_out[n, f]

    send_att(0, o)

    pl.loop(0, 2)(lambda i: forward(5 * c + i))

    def lane(j):
        if j == 0:
            return w0, x, y, lambda at: dev(at, y, z, c)
        return w1, y, x, lambda at: dev(x, at, z, c)

    def pass_on(j, k):
        ref, me, _, at = lane(j)
        for s in (1, 3):
            rcopy(
                ref.at[me, k], ref.at[me, k], a2_ssem.at[j, s, k], a2_rsem.at[j, me, k],
                at((me + s) % 4),
            ).start()

    def relay(e):
        for j in range(2):
            ref, me, first, at = lane(j)
            k = (first + e) % 4
            ahead_by = 1 if e % 2 == 0 else 3
            behind = (me + 4 - ahead_by) % 4
            block = ref.at[behind, k]
            rcopy(block, block, a2_ssem.at[j, 2, k], a2_rsem.at[j, behind, k], sibling).wait_recv()
            rcopy(
                block, block, a2_ssem.at[j, 2, k], a2_rsem.at[j, behind, k],
                at((me + ahead_by) % 4),
            ).start()

    @pl.when(root)
    def _():
        pltpu.make_async_copy(w_mine, w0_mine, own_sem).wait()

    @pl.when(z != 4 * c + h)
    def _():
        rcopy(w0_mine, w0_mine, az_ssem.at[0], az_rsem.at[0], sibling).wait_recv()

    for s in (1, 3, 2):
        rcopy(
            w0_mine, w0_mine, a1_ssem.at[0, s], a1_rsem.at[0, y], dev(x, (y + s) % NY, z, c)
        ).start()
    pass_on(0, y)

    @pl.when(z != 4 * c + 2 + h)
    def _():
        rcopy(w1_mine, w1_mine, az_ssem.at[0], az_rsem.at[1], sibling).wait_recv()

    for s in (1, 3, 2):
        rcopy(
            w1_mine, w1_mine, a1_ssem.at[1, s], a1_rsem.at[1, x], dev((x + s) % NX, y, z, c)
        ).start()
    pass_on(1, x)

    pl.loop(2, 5)(lambda i: forward(5 * c + i))
    send_att(1, c)

    dest_f = dest.astype(F32)
    owner = fdiv(dest_f, OWN)
    owner_col = jnp.sum(
        jnp.where(row_i == col_i, jnp.broadcast_to(owner, (TOK, TOK)), 0.0),
        axis=1, keepdims=True,
    )
    ahead = jnp.where(jnp.logical_and(owner_col == owner, row_i < col_i), 1.0, 0.0)
    position = owner * CAP + jnp.sum(ahead, axis=0, keepdims=True)
    p_pos = p_dev * CAP + p_rank
    for k in range(5):
        h_tok[:, TOK * k : TOK * (k + 1)] = jnp.where(
            jnp.where(p_pair == k, p_pos, -1.0) == position, 1.0, 0.0
        ).astype(BF16)

    for s in (1, 3, 2):
        ys, xs = (y + s) % NY, (x + s) % NX
        rcopy(w0.at[x, ys], w0.at[x, ys], a1_ssem.at[0, s], a1_rsem.at[0, ys], sibling).wait_recv()
        pass_on(0, ys)
        rcopy(w1.at[y, xs], w1.at[y, xs], a1_ssem.at[1, s], a1_rsem.at[1, xs], sibling).wait_recv()
        pass_on(1, xs)

    relay(0)

    def take_att(n):
        @pl.loop(1, NF)
        def _(s):
            frm = (f + s) % NF
            rcopy(
                att_out.at[n, frm], att_in.at[n, frm], c_ssem.at[n, s], c_rsem.at[n, frm], sibling
            ).wait_recv()

        out = dot_tn(att_in[n].reshape(NF * BLK, 128), h_tok[...]).astype(BF16)
        return jnp.concatenate([out[:, TOK * k : TOK * (k + 1)] for k in range(5)], axis=0)

    att_t[...] = take_att(0)
    att_copy = rcopy(att_t, att_all.at[c], sib_ssem.at[0], sib_rsem.at[0], sibling)
    att_copy.start()
    relay(1)
    att_all[c] = take_att(1)
    relay(3)
    loads[3].wait()
    rcopy(cot_hbm, c_all.at[o], sib_ssem.at[1], sib_rsem.at[1], sibling).wait_recv()
    rcopy(att_t, att_all.at[o], sib_ssem.at[0], sib_rsem.at[0], sibling).wait_recv()

    def sums_lane(j):
        if j == 0:
            return s0, r0, x, y, lambda at: dev(at, y, z, c)
        return s1, r1, y, x, lambda at: dev(x, at, z, c)

    def far_out(j, e):
        own, _, me, first, at = sums_lane(j)
        k = (first + e) % 4
        ahead_by = 1 if e % 2 == 0 else 3
        rcopy(
            own.at[(me + 2) % 4, k], m_in.at[j, k], m_ssem.at[j, k], m_rsem.at[j, k],
            at((me + ahead_by) % 4),
        ).start()

    def near_out(j, e):
        own, ins, me, first, at = sums_lane(j)
        k = (first + e) % 4
        behind = (me + (3 if e % 2 == 0 else 1)) % 4
        rcopy(
            own.at[behind, k], ins.at[me, k], b2_ssem.at[j, 0, k], b2_rsem.at[j, me, k], at(behind)
        ).start()

    def sum_out(j, e):
        own, ins, me, first, at = sums_lane(j)
        k = (first + e) % 4
        to = (me + (1 if e % 2 == 0 else 3)) % 4
        rcopy(m_in.at[j, k], m_in.at[j, k], m_ssem.at[j, k], m_rsem.at[j, k], sibling).wait_recv()
        m_out[j, k] = (own[to, k].astype(F32) + m_in[j, k].astype(F32)).astype(BF16)
        rcopy(
            m_out.at[j, k], ins.at[me, k], b2_ssem.at[j, 1, k], b2_rsem.at[j, me, k], at(to)
        ).start()

    att_both = jnp.concatenate([att_all[0], att_all[1]], axis=1)
    for s in (2, 1, 3, 0):
        xs = (x + s) % NX
        cols = c_all[:, :, pl.ds(pl.multiple_of(xs * QD, 128), QD)].reshape(2 * TOK, QD)
        share = dot_nn(att_both, cols)
        for ys in range(NY):
            n = row_of(ys, 0)
            s0[xs, ys] = share[ROWS * n : ROWS * (n + 1)].astype(BF16)
            n = row_of(ys, 1)
            s1[ys, xs] = share[ROWS * n : ROWS * (n + 1)].astype(BF16)
        far_out(1, s)
        if s == 2:
            for e in (2, 1, 3, 0):
                far_out(0, e)
        if s % 2:
            for e in (2, 0) if s == 3 else (1, 3):
                near_out(0, e)
        near_out(1, s)
    relay(2)
    for e in (2, 1, 3, 0):
        for j in range(2):
            sum_out(j, e)

    for e in range(4):
        for j in range(2):
            ref, me, first, _ = lane(j)
            k = (first + e) % 4
            for s in (1 if e % 2 == 0 else 3, 2):
                block = ref.at[(me + s) % 4, k]
                rcopy(
                    block, block, a2_ssem.at[j, s, k], a2_rsem.at[j, (me + s) % 4, k], sibling
                ).wait_recv()
    total = None
    for k in range(4):
        blocks = []
        for n in range(8):
            ys, j = n % 4, n // 4
            blocks.append(w0[k, ys] if j == 0 else w1[ys, k])
        wk = jnp.concatenate(blocks, axis=0)
        cols = c_all[:, :, QD * k : QD * (k + 1)].reshape(2 * TOK, QD)
        term = dot_nt(cols, wk)
        total = term if total is None else total + term
    total = total.astype(BF16)
    for g in range(2):
        for i in range(5):
            g_tmp[g, i] = total[TOK * g : TOK * (g + 1), 128 * i : 128 * (i + 1)]
    g_copy = rcopy(g_tmp.at[o], g_tok, sib_ssem.at[2], sib_rsem.at[2], sibling)
    g_copy.start()

    def send_grad(n, rows):
        g_out[n] = dot_nn(h_tok[...], rows.reshape(5 * TOK, 128)).astype(BF16).reshape(NF, BLK, 128)

        @pl.loop(1, NF)
        def _(s):
            to = (f + s) % NF
            rcopy(
                g_out.at[n, to], g_in.at[n, f], g_ssem.at[n, s], g_rsem.at[n, f], (dp, to)
            ).start()

        g_in[n, f] = g_out[n, f]

    send_grad(0, g_tmp[c])
    rcopy(g_tmp.at[o], g_tok, sib_ssem.at[2], sib_rsem.at[2], sibling).wait_recv()
    send_grad(1, g_tok[...])

    for e in (2, 1, 3, 0):
        for j in range(2):
            if j == 0:
                own, ins, out, nxt, me, k = s0, r0, t0, u0, x, (y + e) % NY
                after, to = y, dev(x, k, z, c)
            else:
                own, ins, out, nxt, me, k = s1, r1, t1, u1, y, (x + e) % NX
                after, to = x, dev(k, y, z, c)
            acc = own[me, k].astype(F32)
            for s in (1, 3):
                frm = (me + s) % 4
                rcopy(
                    own.at[frm, k], ins.at[frm, k], b2_ssem.at[j, 0, 0], b2_rsem.at[j, frm, k],
                    sibling,
                ).wait_recv()
                acc += ins[frm, k].astype(F32)
            if e:
                out[k] = acc.astype(BF16)
                rcopy(
                    out.at[k], nxt.at[after], b1_ssem.at[j, e], b1_rsem.at[j, after], to
                ).start()
            else:
                vf[j] = acc

    for j, (me, src, dst) in enumerate(((y, t0, u0), (x, t1, u1))):
        acc = vf[j]
        for s in range(1, 4):
            frm = (me + s) % 4
            rcopy(
                src.at[frm], dst.at[frm], b1_ssem.at[j, s], b1_rsem.at[j, frm], sibling
            ).wait_recv()
            acc += dst[frm].astype(F32)
        vf[j] = acc
        vb[j] = acc.astype(BF16)
        z_root = 4 * c + 2 * j + h

        @pl.when(z != z_root)
        def _(j=j, z_root=z_root):
            rcopy(
                vb.at[j], zr.at[z], bz_ssem.at[j], bz_rsem.at[z], dev(x, y, z_root, c)
            ).start()

    def take_grad(n):
        @pl.loop(1, NF)
        def _(s):
            frm = (f + s) % NF
            rcopy(
                g_out.at[n, frm], g_in.at[n, frm], g_ssem.at[n, s], g_rsem.at[n, frm], sibling
            ).wait_recv()

        out = dot_tn(g_in[n].reshape(NF * BLK, 128), h_own[...])
        for k in range(5):
            g_v[k] = out[:, SPAD * k : SPAD * (k + 1)].T[:OWN].astype(BF16)

    live = ids_col >= 0.0

    def backward(p, gp):
        at = pl.ds(pl.multiple_of(p * 128, 128), 128)
        qp, kp, vp = q_v[:, at], k_v[:, at], v_v[:, at]
        prob = probs[p]
        pg = dot_nt(both_heads(gp), vp)
        delta = jnp.sum(prob * pg, axis=1, keepdims=True)
        sg = (prob * (pg - delta)).astype(BF16)
        pb = prob.astype(BF16)
        dq = dot_nn(sg, kp)

        def put(ref, one, two, scale):
            value = jnp.where(first_head, one, two) * scale
            ref[:, at] = jnp.where(live, value, 0.0).astype(BF16)

        put(dq_v, dq[:OWN], dq[OWN:], SCALE)
        put(dk_v, dot_tn(sg[:OWN], qp), dot_tn(sg[OWN:], qp), SCALE)
        put(dv_v, dot_tn(pb[:OWN], gp), dot_tn(pb[OWN:], gp), 1.0)

    take_grad(0)
    pl.loop(0, 5)(lambda i: backward(5 * c + i, g_v[i]))
    take_grad(1)
    pl.loop(0, 5)(lambda i: backward(5 * o + i, g_v[i]))
    outs = [
        pltpu.make_async_copy(src, dst, out_sem.at[i])
        for i, (src, dst) in enumerate(((dq_v, dq_hbm), (dk_v, dk_hbm), (dv_v, dv_hbm)))
    ]
    for out in outs:
        out.start()

    def emit(i):
        pltpu.make_async_copy(
            fall.at[i],
            wg_hbm.at[:, pl.ds(pl.multiple_of(i * QD, 128), QD)],
            wg_sem.at[i],
        ).start()

    def to_sibling(i):
        rcopy(fall.at[i], fall.at[i], f3_ssem.at[i], f3_rsem.at[i], sibling).start()
        emit(i)

    @pl.when(root)
    def _():
        acc = vf[root_j]
        for s in range(1, NZ):
            frm = (z + s) % NZ
            rcopy(vb.at[0], zr.at[frm], bz_ssem.at[0], bz_rsem.at[frm], sibling).wait_recv()
            acc += zr[frm].astype(F32)
        fall[x] = acc.astype(BF16)
        for s in (1, 3, 2, 0):
            for e in (2, 0):
                if s or e:
                    rcopy(
                        fall.at[x], fall.at[x], f2_ssem.at[s, e // 2], f2_rsem.at[x],
                        dev((x + s) % NX, (y + e) % NY, z, c),
                    ).start()
        to_sibling(x)

    @pl.when(jnp.logical_and(active, z % 2 != h))
    def _():
        rcopy(fall.at[x], fall.at[x], f2_ssem.at[0, 0], f2_rsem.at[x], sibling).wait_recv()
        to_sibling(x)

    @pl.when(active)
    def _():
        for s in (1, 3, 2):
            xs = (x + s) % NX
            rcopy(fall.at[xs], fall.at[xs], f2_ssem.at[0, 0], f2_rsem.at[xs], sibling).wait_recv()
            to_sibling(xs)

    @pl.when(jnp.logical_not(active))
    def _():
        for s in (0, 1, 3, 2):
            xs = (x + s) % NX
            rcopy(
                fall.at[xs], fall.at[xs], f3_ssem.at[xs], f3_rsem.at[xs], sibling
            ).wait_recv()
            emit(xs)

    @pl.when(root)
    def _():
        @pl.loop(1, NZ)
        def _(s):
            rcopy(w_mine, w0_mine, az_ssem.at[s], az_rsem.at[0], sibling).wait_send()

        for s in range(4):
            for e in range(2):
                if s or e:
                    rcopy(
                        fall.at[x], fall.at[x], f2_ssem.at[s, e], f2_rsem.at[x], sibling
                    ).wait_send()

    @pl.loop(1, NF)
    def _(s):
        rcopy(dsend, drecv.at[f], d_ssem.at[s], d_rsem.at[f], sibling).wait_send()
        for n in range(2):
            rcopy(
                att_out.at[n, f], att_in.at[n, f], c_ssem.at[n, s], c_rsem.at[n, f], sibling
            ).wait_send()
            rcopy(
                g_out.at[n, f], g_in.at[n, f], g_ssem.at[n, s], g_rsem.at[n, f], sibling
            ).wait_send()

    for s in range(1, 4):
        for j, w in enumerate((w0_mine, w1_mine)):
            rcopy(w, w, a1_ssem.at[j, s], a1_rsem.at[j, 0], sibling).wait_send()
        for k in range(4):
            for j in range(2):
                rcopy(
                    w0_mine, w0_mine, a2_ssem.at[j, s, k], a2_rsem.at[j, 0, 0], sibling
                ).wait_send()
        for j, w in enumerate((t0.at[y], t1.at[x])):
            rcopy(w, w, b1_ssem.at[j, s], b1_rsem.at[j, 0], sibling).wait_send()
    for j in range(2):
        for k in range(4):
            block = m_in.at[j, k]
            rcopy(block, block, m_ssem.at[j, k], m_rsem.at[j, k], sibling).wait_send()
            for s in range(2):
                rcopy(block, block, b2_ssem.at[j, s, k], m_rsem.at[j, k], sibling).wait_send()
    att_copy.wait_send()
    c_copy.wait_send()
    g_copy.wait_send()
    for j in range(2):

        @pl.when(z != 4 * c + 2 * j + h)
        def _(j=j):
            rcopy(vb.at[j], zr.at[z], bz_ssem.at[j], bz_rsem.at[z], sibling).wait_send()

    @pl.when(active)
    def _():
        for s in range(4):
            rcopy(fall.at[s], fall.at[s], f3_ssem.at[s], f3_rsem.at[s], sibling).wait_send()

    for out in outs:
        out.wait()
    for i in range(4):
        pltpu.make_async_copy(
            fall.at[i], wg_hbm.at[:, QD * i : QD * (i + 1)], wg_sem.at[i]
        ).wait()


def finish(dq_in, dk_in, dv_in, wg_in, dq_out, dk_out, dv_out, wg_out, grads, wg_b, wg_f, sems):
    pairs = ((dq_in, dq_out), (dk_in, dk_out), (dv_in, dv_out))
    reads = [pltpu.make_async_copy(pairs[i][0], grads.at[i], sems.at[i]) for i in range(3)]
    reads.append(pltpu.make_async_copy(wg_in, wg_b, sems.at[3]))
    writes = [pltpu.make_async_copy(grads.at[i], pairs[i][1], sems.at[i]) for i in range(3)]
    writes.append(pltpu.make_async_copy(wg_f, wg_out, sems.at[3]))
    for read in reads:
        read.start()
    for i in range(3):
        reads[i].wait()
        writes[i].start()
    reads[3].wait()
    wg_f[...] = wg_b[...].astype(F32)
    for write in writes[3:]:
        write.start()
    for write in writes:
        write.wait()


def per_device(cotangent, out_weight, queries, key_vectors, value_vectors, destination, protein_ids):
    dma = pltpu.SemaphoreType.DMA
    vmem = pltpu.VMEM
    slots = jax.ShapeDtypeStruct((OWN, PAIRS * 128), BF16)
    any_space = pl.BlockSpec(memory_space=pl.ANY)
    in_vmem = pl.BlockSpec(memory_space=pltpu.VMEM)
    *grads, weight_grad = pl.pallas_call(
        kernel,
        out_shape=(slots, slots, slots, jax.ShapeDtypeStruct((ROWS, D), BF16)),
        in_specs=[any_space] * 5 + [in_vmem] * 2,
        out_specs=(any_space,) * 4,
        scratch_shapes=[
            *[vmem((OWN, PAIRS * 128), BF16) for _ in range(6)],
            vmem((8, TOK), jnp.int32),
            vmem((NF, 8, TOK), jnp.int32),
            vmem((2, TOK, D), BF16),
            vmem((NF * BLK, 5 * SPAD), BF16),
            vmem((NF * BLK, 5 * TOK), BF16),
            vmem((PAIRS, SPAD, 128), BF16),
            vmem((2, NF, BLK, 128), BF16),
            vmem((2, NF, BLK, 128), BF16),
            vmem((640, TOK), BF16),
            vmem((2, 640, TOK), BF16),
            vmem((PAIRS, 2 * OWN, OWN), F32),
            vmem((OWN, OWN), F32),
            vmem((NX, NY, ROWS, QD), BF16),
            vmem((NY, NX, ROWS, QD), BF16),
            vmem((2, 5, TOK, 128), BF16),
            vmem((5, TOK, 128), BF16),
            vmem((2, NF, BLK, 128), BF16),
            vmem((2, NF, BLK, 128), BF16),
            vmem((5, OWN, 128), BF16),
            *[vmem((4, 4, ROWS, QD), BF16) for _ in range(4)],
            *[vmem((2, 4, ROWS, QD), BF16) for _ in range(2)],
            *[vmem((4, ROWS, QD), BF16) for _ in range(4)],
            vmem((2, ROWS, QD), F32),
            vmem((2, ROWS, QD), BF16),
            vmem((NZ, ROWS, QD), BF16),
            vmem((NX, ROWS, QD), BF16),
            dma((4,)), dma((3,)), dma((4,)), dma,
            dma((NF,)), dma((NF,)), *[dma((2, NF)) for _ in range(4)],
            dma((NZ,)), dma((2,)), dma((2, 4)), dma((2, 4)), dma((2, 4, 4)), dma((2, 4, 4)),
            dma((3,)), dma((3,)),
            dma((2, 4)), dma((2, 4)), dma((2, 2, 4)), dma((2, 4, 4)),
            dma((2, 4)), dma((2, 4)), dma((2,)), dma((NZ,)),
            dma((4, 2)), dma((4,)), dma((4,)), dma((4,)),
        ],
        compiler_params=pltpu.CompilerParams(
            collective_id=0, has_side_effects=True, vmem_limit_bytes=56 * 1024 * 1024
        ),
    )(
        cotangent, out_weight, queries, key_vectors, value_vectors,
        destination.reshape(1, TOK), protein_ids.reshape(1, OWN),
    )
    return pl.pallas_call(
        finish,
        out_shape=(slots, slots, slots, jax.ShapeDtypeStruct((ROWS, D), F32)),
        in_specs=[any_space] * 4,
        out_specs=(any_space,) * 4,
        scratch_shapes=[vmem((3, OWN, PAIRS * 128), BF16), vmem((ROWS, D), BF16), vmem((ROWS, D), F32), dma((4,))],
    )(*grads, weight_grad)


def solution(mesh):
    rows = P(("dp", "fsdp"), None)
    return jax.shard_map(
        per_device,
        mesh=mesh,
        in_specs=(rows, P("fsdp", None), rows, rows, rows, P(("dp", "fsdp")), P(("dp", "fsdp"))),
        out_specs=(rows, rows, rows, P("fsdp", None)),
        check_vma=False,
    )
```

```python
import jax
import jax.numpy as jnp
from jax import lax
from jax.experimental import pallas as pl
from jax.experimental.pallas import tpu as pltpu
from jax.sharding import PartitionSpec as P

F32 = jnp.float32
BF16 = jnp.bfloat16
MESH = pl.DeviceIdType.MESH

NX, NY, NZ, NF = 4, 4, 8, 16
TOK = 128
OWN = 192
CAP = 12
D = 2560
QD = D // 4
ROWS = 80
GATHER = ((0, 32), (32, 48))
SPREAD = ((0, 48), (48, 32))
BLK = 64
SPAD = 256
PAIRS = 10
SCALE = 0.125


def fdiv(values, by):
    return jnp.floor((values + 0.5) * (1.0 / by))


def iota(shape, dim):
    return lax.broadcasted_iota(jnp.int32, shape, dim).astype(F32)


def dot_nt(a, b):
    return lax.dot_general(a, b, (((1,), (1,)), ((), ())), preferred_element_type=F32)


def dot_tn(a, b):
    return lax.dot_general(a, b, (((0,), (0,)), ((), ())), preferred_element_type=F32)


def dot_nn(a, b):
    return jnp.dot(a, b, preferred_element_type=F32)


def row_of(y, j):
    return 4 * j + y


def kernel(
    cot_hbm, w_hbm, q_hbm, k_hbm, v_hbm, dest_ref, ids_ref,
    dq_hbm, dk_hbm, dv_hbm, wg_hbm,
    q_v, k_v, v_v, dq_v, dk_v, dv_v,
    dsend, drecv, c_all, h_own, h_tok,
    att, att_out, att_in, att_t, att_all, probs, same_v,
    w0, w1, g_tmp, g_tok, g_out, g_in, g_v,
    s0, s1, r0, r1, m_in, m_out, t0, t1, u0, u1, vf, vb, zr, fall,
    load_sem, out_sem, wg_sem, own_sem,
    d_ssem, d_rsem, c_ssem, c_rsem, g_ssem, g_rsem,
    az_ssem, az_rsem, a1_ssem, a1_rsem, a2_ssem, a2_rsem,
    sib_ssem, sib_rsem,
    m_ssem, m_rsem, b2_ssem, b2_rsem, b1_ssem, b1_rsem, bz_ssem, bz_rsem,
    f2_ssem, f2_rsem, f3_ssem, f3_rsem,
):
    dp = lax.axis_index("dp")
    f = lax.axis_index("fsdp")
    c = dp % 2
    x = (dp // 2) % NX
    h = dp // 8
    z = f // 2
    y = 2 * h + f % 2
    o = 1 - c

    def dev(x_, y_, z_, c_):
        return (((y_ // 2) * NX + x_) * 2 + c_, z_ * 2 + y_ % 2)

    def rcopy(src, dst, ssem, rsem, target):
        return pltpu.make_async_remote_copy(
            src_ref=src, dst_ref=dst, send_sem=ssem, recv_sem=rsem,
            device_id=target, device_id_type=MESH,
        )

    sibling = dev(x, y, z, o)

    loads = [
        pltpu.make_async_copy(src, dst, load_sem.at[i])
        for i, (src, dst) in enumerate(
            ((q_hbm, q_v), (k_hbm, k_v), (v_hbm, v_v), (cot_hbm, c_all.at[c]))
        )
    ]
    for load in loads:
        load.start()

    barrier = pltpu.get_barrier_semaphore()

    @pl.loop(1, NF)
    def _(s):
        pl.semaphore_signal(
            barrier, inc=1, device_id=(dp, (f + s) % NF), device_id_type=MESH
        )

    for s in range(1, 4):
        pl.semaphore_signal(
            barrier, inc=1, device_id=dev((x + s) % NX, y, z, c), device_id_type=MESH
        )
        pl.semaphore_signal(
            barrier, inc=1, device_id=dev(x, (y + s) % NY, z, c), device_id_type=MESH
        )
        pl.semaphore_signal(
            barrier, inc=1, device_id=dev((x + s) % NX, (y + 2) % NY, z, c), device_id_type=MESH
        )
    pl.semaphore_signal(barrier, inc=1, device_id=sibling, device_id_type=MESH)

    ids = ids_ref[...].astype(F32)
    srow = iota((OWN, OWN), 0)
    scol = iota((OWN, OWN), 1)
    ids_col = jnp.sum(
        jnp.where(srow == scol, jnp.broadcast_to(ids, (OWN, OWN)), 0.0), axis=1, keepdims=True
    )
    same_v[...] = jnp.where(ids_col == ids, 1.0, 0.0)
    dest = dest_ref[...]
    dsend[...] = jnp.broadcast_to(dest, (8, TOK))
    att[:, OWN:SPAD] = jnp.zeros((PAIRS, SPAD - OWN, 128), BF16)
    lane = lax.broadcasted_iota(jnp.int32, (1, 128), 1)
    head_masks = (
        jnp.where(lane < 64, 1.0, 0.0).astype(BF16),
        jnp.where(lane < 64, 0.0, 1.0).astype(BF16),
    )
    first_head = lax.broadcasted_iota(jnp.int32, (OWN, 128), 1) < 64

    def both_heads(rows):
        return jnp.concatenate([rows * head_masks[0], rows * head_masks[1]], axis=0)

    def forward(p):
        at = pl.ds(pl.multiple_of(p * 128, 128), 128)
        qp, kp, vp = q_v[:, at], k_v[:, at], v_v[:, at]
        scores = dot_nt(both_heads(qp), kp) * SCALE
        same = jnp.concatenate([same_v[...], same_v[...]], axis=0)
        scores = jnp.where(same > 0.0, scores, -1e30)
        top = jnp.max(scores, axis=1, keepdims=True)
        e = jnp.exp(scores - top)
        prob = e * (1.0 / jnp.sum(e, axis=1, keepdims=True))
        probs[p] = prob
        out = dot_nn(prob.astype(BF16), vp)
        att[p, 0:OWN] = jnp.where(first_head, out[:OWN], out[OWN:]).astype(BF16)

    for load in loads[:3]:
        load.wait()
    pl.loop(0, 2)(lambda i: forward(5 * o + i))
    pl.semaphore_wait(barrier, 25)

    @pl.loop(1, NF)
    def _(s):
        rcopy(dsend, drecv.at[f], d_ssem.at[s], d_rsem.at[f], (dp, (f + s) % NF)).start()

    drecv[f] = dsend[...]

    active = z // 4 == c
    root = jnp.logical_and(active, z % 2 == h)
    root_j = (z % 4) // 2
    w_mine = w_hbm.at[:, pl.ds(pl.multiple_of(x * QD, 128), QD)]

    def spread_z(dst):
        for q, rows in enumerate(GATHER):
            src, to = w_mine.at[pl.ds(*rows)], dst.at[pl.ds(*rows)]
            pltpu.make_async_copy(src, to, own_sem.at[q]).start()

            @pl.loop(1, NZ)
            def _(s, q=q, src=src, to=to):
                rcopy(
                    src, to, az_ssem.at[s, q], az_rsem.at[root_j, q], dev(x, y, (z + s) % NZ, c)
                ).start()

    w0_mine = w0.at[x, y]
    w1_mine = w1.at[y, x]

    @pl.when(jnp.logical_and(root, root_j == 0))
    def _():
        spread_z(w0_mine)

    @pl.when(jnp.logical_and(root, root_j == 1))
    def _():
        spread_z(w1_mine)

    c_copy = rcopy(cot_hbm, c_all.at[c], sib_ssem.at[1], sib_rsem.at[1], sibling)
    c_copy.start()

    pl.loop(2, 5)(lambda i: forward(5 * o + i))

    @pl.loop(1, NF)
    def _(s):
        frm = (f + s) % NF
        rcopy(dsend, drecv.at[frm], d_ssem.at[s], d_rsem.at[frm], sibling).wait_recv()

    row_i = iota((TOK, TOK), 0)
    col_i = iota((TOK, TOK), 1)
    p_col = iota((NF * BLK, 1), 0)
    p_dev = fdiv(p_col, BLK)
    p_in = p_col - p_dev * BLK
    p_pair = fdiv(p_in, CAP)
    p_rank = p_in - p_pair * CAP
    dests = jnp.concatenate([drecv[k][0:1] for k in range(NF)], axis=0).astype(F32)
    owners = fdiv(dests, OWN)
    here = owners == f.astype(F32)
    before = jnp.where(row_i < col_i, 1.0, 0.0).astype(BF16)
    ranks = dot_nn(jnp.where(here, 1.0, 0.0).astype(BF16), before)
    ranks = jnp.where(here, ranks, -1.0).astype(BF16)
    slots = (dests - owners * OWN).astype(BF16)
    source = jnp.where(p_dev == iota((NF * BLK, NF), 1), 1.0, 0.0).astype(BF16)
    slot_col = jnp.sum(
        jnp.where(dot_nn(source, ranks) == p_rank, dot_nn(source, slots) + 1.0, 0.0),
        axis=1, keepdims=True,
    )
    slot_lane = iota((1, SPAD), 1) + 1.0
    for k in range(5):
        h_own[:, SPAD * k : SPAD * (k + 1)] = jnp.where(
            jnp.where(p_pair == k, slot_col, 0.0) == slot_lane, 1.0, 0.0
        ).astype(BF16)

    def send_att(n, part):
        rows = att[pl.ds(5 * part, 5)].reshape(5 * SPAD, 128)
        att_out[n] = dot_nn(h_own[...], rows).astype(BF16).reshape(NF, BLK, 128)

        @pl.loop(1, NF)
        def _(s):
            to = (f + s) % NF
            rcopy(
                att_out.at[n, to], att_in.at[n, f], c_ssem.at[n, s], c_rsem.at[n, f], (dp, to)
            ).start()

        att_in[n, f] = att_out[n, f]

    send_att(0, o)


    def lane(j):
        if j == 0:
            return w0, x, y, lambda at: dev(at, y, z, c)
        return w1, y, x, lambda at: dev(x, at, z, c)

    def pass_on(j, k, q):
        ref, me, _, at = lane(j)
        piece = ref.at[me, k, pl.ds(*GATHER[q])]
        for s in (1, 3):
            rcopy(
                piece, piece, a2_ssem.at[j, s, k, q], a2_rsem.at[j, me, k, q], at((me + s) % 4)
            ).start()

    def relay(e):
        for q, rows in enumerate(GATHER):
            for j in range(2):
                ref, me, first, at = lane(j)
                k = (first + e) % 4
                ahead_by = 1 if e % 2 == 0 else 3
                behind = (me + 4 - ahead_by) % 4
                piece = ref.at[behind, k, pl.ds(*rows)]
                sems = a2_ssem.at[j, 2, k, q], a2_rsem.at[j, behind, k, q]
                rcopy(piece, piece, *sems, sibling).wait_recv()
                rcopy(piece, piece, *sems, at((me + ahead_by) % 4)).start()

    def begin(q):
        rows = pl.ds(*GATHER[q])

        @pl.when(root)
        def _():
            pltpu.make_async_copy(w_mine.at[rows], w0_mine.at[rows], own_sem.at[q]).wait()

        for j, mine in enumerate((w0_mine, w1_mine)):
            piece = mine.at[rows]

            @pl.when(z != 4 * c + 2 * j + h)
            def _(j=j, piece=piece):
                rcopy(piece, piece, az_ssem.at[0, q], az_rsem.at[j, q], sibling).wait_recv()

            me = y if j == 0 else x
            for s in (1, 3, 2):
                to = dev(x, (y + s) % NY, z, c) if j == 0 else dev((x + s) % NX, y, z, c)
                rcopy(piece, piece, a1_ssem.at[j, s, q], a1_rsem.at[j, me, q], to).start()
            pass_on(j, me, q)

    begin(0)
    pl.loop(0, 2)(lambda i: forward(5 * c + i))
    begin(1)
    pl.loop(2, 5)(lambda i: forward(5 * c + i))
    send_att(1, c)

    dest_f = dest.astype(F32)
    owner = fdiv(dest_f, OWN)
    owner_col = jnp.sum(
        jnp.where(row_i == col_i, jnp.broadcast_to(owner, (TOK, TOK)), 0.0),
        axis=1, keepdims=True,
    )
    ahead = jnp.where(jnp.logical_and(owner_col == owner, row_i < col_i), 1.0, 0.0)
    position = owner * CAP + jnp.sum(ahead, axis=0, keepdims=True)
    p_pos = p_dev * CAP + p_rank
    for k in range(5):
        h_tok[:, TOK * k : TOK * (k + 1)] = jnp.where(
            jnp.where(p_pair == k, p_pos, -1.0) == position, 1.0, 0.0
        ).astype(BF16)

    for s in (1, 3, 2):
        ys, xs = (y + s) % NY, (x + s) % NX
        for q, rows in enumerate(GATHER):
            for j, ref, k in ((0, w0.at[x, ys], ys), (1, w1.at[y, xs], xs)):
                piece = ref.at[pl.ds(*rows)]
                rcopy(piece, piece, a1_ssem.at[j, s, q], a1_rsem.at[j, k, q], sibling).wait_recv()
                pass_on(j, k, q)

    relay(0)

    def take_att(n):
        @pl.loop(1, NF)
        def _(s):
            frm = (f + s) % NF
            rcopy(
                att_out.at[n, frm], att_in.at[n, frm], c_ssem.at[n, s], c_rsem.at[n, frm], sibling
            ).wait_recv()

        out = dot_tn(att_in[n].reshape(NF * BLK, 128), h_tok[...]).astype(BF16)
        return jnp.concatenate([out[:, TOK * k : TOK * (k + 1)] for k in range(5)], axis=0)

    att_t[...] = take_att(0)
    att_copy = rcopy(att_t, att_all.at[c], sib_ssem.at[0], sib_rsem.at[0], sibling)
    att_copy.start()
    relay(1)
    att_all[c] = take_att(1)
    relay(3)
    loads[3].wait()
    rcopy(cot_hbm, c_all.at[o], sib_ssem.at[1], sib_rsem.at[1], sibling).wait_recv()
    rcopy(att_t, att_all.at[o], sib_ssem.at[0], sib_rsem.at[0], sibling).wait_recv()

    def sums_lane(j):
        if j == 0:
            return s0, r0, x, y, lambda at: dev(at, y, z, c)
        return s1, r1, y, x, lambda at: dev(x, at, z, c)

    def far_out(j, e):
        own, _, me, first, at = sums_lane(j)
        k = (first + e) % 4
        ahead_by = 1 if e % 2 == 0 else 3
        rcopy(
            own.at[(me + 2) % 4, k], m_in.at[j, k], m_ssem.at[j, k], m_rsem.at[j, k],
            at((me + ahead_by) % 4),
        ).start()

    def near_out(j, e):
        own, ins, me, first, at = sums_lane(j)
        k = (first + e) % 4
        behind = (me + (3 if e % 2 == 0 else 1)) % 4
        rcopy(
            own.at[behind, k], ins.at[me, k], b2_ssem.at[j, 0, k], b2_rsem.at[j, me, k], at(behind)
        ).start()

    def sum_out(j, e):
        own, ins, me, first, at = sums_lane(j)
        k = (first + e) % 4
        to = (me + (1 if e % 2 == 0 else 3)) % 4
        rcopy(m_in.at[j, k], m_in.at[j, k], m_ssem.at[j, k], m_rsem.at[j, k], sibling).wait_recv()
        m_out[j, k] = (own[to, k].astype(F32) + m_in[j, k].astype(F32)).astype(BF16)
        rcopy(
            m_out.at[j, k], ins.at[me, k], b2_ssem.at[j, 1, k], b2_rsem.at[j, me, k], at(to)
        ).start()

    att_both = jnp.concatenate([att_all[0], att_all[1]], axis=1)
    for s in (2, 1, 3, 0):
        xs = (x + s) % NX
        cols = c_all[:, :, pl.ds(pl.multiple_of(xs * QD, 128), QD)].reshape(2 * TOK, QD)
        share = dot_nn(att_both, cols)
        for ys in range(NY):
            n = row_of(ys, 0)
            s0[xs, ys] = share[ROWS * n : ROWS * (n + 1)].astype(BF16)
            n = row_of(ys, 1)
            s1[ys, xs] = share[ROWS * n : ROWS * (n + 1)].astype(BF16)
        far_out(1, s)
        if s == 2:
            for e in (2, 1, 3, 0):
                far_out(0, e)
        if s % 2:
            for e in (2, 0) if s == 3 else (1, 3):
                near_out(0, e)
        near_out(1, s)
    relay(2)
    for e in (2, 1, 3, 0):
        for j in range(2):
            sum_out(j, e)

    for e in range(4):
        for j in range(2):
            ref, me, first, _ = lane(j)
            k = (first + e) % 4
            for s in (1 if e % 2 == 0 else 3, 2):
                for q, rows in enumerate(GATHER):
                    piece = ref.at[(me + s) % 4, k, pl.ds(*rows)]
                    rcopy(
                        piece, piece, a2_ssem.at[j, s, k, q], a2_rsem.at[j, (me + s) % 4, k, q],
                        sibling,
                    ).wait_recv()
    total = None
    for k in range(4):
        blocks = []
        for n in range(8):
            ys, j = n % 4, n // 4
            blocks.append(w0[k, ys] if j == 0 else w1[ys, k])
        wk = jnp.concatenate(blocks, axis=0)
        cols = c_all[:, :, QD * k : QD * (k + 1)].reshape(2 * TOK, QD)
        term = dot_nt(cols, wk)
        total = term if total is None else total + term
    total = total.astype(BF16)
    for g in range(2):
        for i in range(5):
            g_tmp[g, i] = total[TOK * g : TOK * (g + 1), 128 * i : 128 * (i + 1)]
    g_copy = rcopy(g_tmp.at[o], g_tok, sib_ssem.at[2], sib_rsem.at[2], sibling)
    g_copy.start()

    def send_grad(n, rows):
        g_out[n] = dot_nn(h_tok[...], rows.reshape(5 * TOK, 128)).astype(BF16).reshape(NF, BLK, 128)

        @pl.loop(1, NF)
        def _(s):
            to = (f + s) % NF
            rcopy(
                g_out.at[n, to], g_in.at[n, f], g_ssem.at[n, s], g_rsem.at[n, f], (dp, to)
            ).start()

        g_in[n, f] = g_out[n, f]

    send_grad(0, g_tmp[c])
    rcopy(g_tmp.at[o], g_tok, sib_ssem.at[2], sib_rsem.at[2], sibling).wait_recv()
    send_grad(1, g_tok[...])

    for e in (2, 1, 3, 0):
        for j in range(2):
            if j == 0:
                own, ins, out, nxt, me, k = s0, r0, t0, u0, x, (y + e) % NY
                after, to = y, dev(x, k, z, c)
            else:
                own, ins, out, nxt, me, k = s1, r1, t1, u1, y, (x + e) % NX
                after, to = x, dev(k, y, z, c)
            acc = own[me, k].astype(F32)
            for s in (1, 3):
                frm = (me + s) % 4
                rcopy(
                    own.at[frm, k], ins.at[frm, k], b2_ssem.at[j, 0, 0], b2_rsem.at[j, frm, k],
                    sibling,
                ).wait_recv()
                acc += ins[frm, k].astype(F32)
            if e:
                out[k] = acc.astype(BF16)
                rcopy(
                    out.at[k], nxt.at[after], b1_ssem.at[j, e], b1_rsem.at[j, after], to
                ).start()
            else:
                vf[j] = acc

    for j, (me, src, dst) in enumerate(((y, t0, u0), (x, t1, u1))):
        acc = vf[j]
        for s in range(1, 4):
            frm = (me + s) % 4
            rcopy(
                src.at[frm], dst.at[frm], b1_ssem.at[j, s], b1_rsem.at[j, frm], sibling
            ).wait_recv()
            acc += dst[frm].astype(F32)
        vf[j] = acc
        vb[j] = acc.astype(BF16)
        z_root = 4 * c + 2 * j + h

        @pl.when(z != z_root)
        def _(j=j, z_root=z_root):
            for q, rows in enumerate(SPREAD):
                rcopy(
                    vb.at[j, pl.ds(*rows)], zr.at[z, pl.ds(*rows)], bz_ssem.at[j, q],
                    bz_rsem.at[z, q], dev(x, y, z_root, c),
                ).start()

    def take_grad(n):
        @pl.loop(1, NF)
        def _(s):
            frm = (f + s) % NF
            rcopy(
                g_out.at[n, frm], g_in.at[n, frm], g_ssem.at[n, s], g_rsem.at[n, frm], sibling
            ).wait_recv()

        out = dot_tn(g_in[n].reshape(NF * BLK, 128), h_own[...])
        for k in range(5):
            g_v[k] = out[:, SPAD * k : SPAD * (k + 1)].T[:OWN].astype(BF16)

    live = ids_col >= 0.0

    def backward(p, gp):
        at = pl.ds(pl.multiple_of(p * 128, 128), 128)
        qp, kp, vp = q_v[:, at], k_v[:, at], v_v[:, at]
        prob = probs[p]
        pg = dot_nt(both_heads(gp), vp)
        delta = jnp.sum(prob * pg, axis=1, keepdims=True)
        sg = (prob * (pg - delta)).astype(BF16)
        pb = prob.astype(BF16)
        dq = dot_nn(sg, kp)

        def put(ref, one, two, scale):
            value = jnp.where(first_head, one, two) * scale
            ref[:, at] = jnp.where(live, value, 0.0).astype(BF16)

        put(dq_v, dq[:OWN], dq[OWN:], SCALE)
        put(dk_v, dot_tn(sg[:OWN], qp), dot_tn(sg[OWN:], qp), SCALE)
        put(dv_v, dot_tn(pb[:OWN], gp), dot_tn(pb[OWN:], gp), 1.0)

    take_grad(0)
    pl.loop(0, 5)(lambda i: backward(5 * c + i, g_v[i]))
    take_grad(1)
    pl.loop(0, 2)(lambda i: backward(5 * o + i, g_v[i]))
    def piece_of(i, q):
        return fall.at[i, pl.ds(*SPREAD[q])]

    def emit(i, q):
        pltpu.make_async_copy(
            piece_of(i, q),
            wg_hbm.at[pl.ds(*SPREAD[q]), pl.ds(pl.multiple_of(i * QD, 128), QD)],
            wg_sem.at[i, q],
        ).start()

    def to_sibling(i, q):
        piece = piece_of(i, q)
        rcopy(piece, piece, f3_ssem.at[i, q], f3_rsem.at[i, q], sibling).start()
        emit(i, q)

    @pl.when(root)
    def _():
        for q, (top, count) in enumerate(SPREAD):
            acc = vf[root_j, top : top + count]
            for s in range(1, NZ):
                frm = (z + s) % NZ
                rows = pl.ds(top, count)
                rcopy(
                    vb.at[0, rows], zr.at[frm, rows], bz_ssem.at[0, q], bz_rsem.at[frm, q], sibling
                ).wait_recv()
                acc += zr[frm, top : top + count].astype(F32)
            fall[x, top : top + count] = acc.astype(BF16)
            piece = piece_of(x, q)
            for s in (1, 3, 2, 0):
                for e in (2, 0):
                    if s or e:
                        rcopy(
                            piece, piece, f2_ssem.at[s, e // 2, q], f2_rsem.at[x, q],
                            dev((x + s) % NX, (y + e) % NY, z, c),
                        ).start()
            to_sibling(x, q)

    pl.loop(2, 5)(lambda i: backward(5 * o + i, g_v[i]))
    outs = [
        pltpu.make_async_copy(src, dst, out_sem.at[i])
        for i, (src, dst) in enumerate(((dq_v, dq_hbm), (dk_v, dk_hbm), (dv_v, dv_hbm)))
    ]
    for out in outs:
        out.start()

    for q in range(2):

        @pl.when(jnp.logical_and(active, z % 2 != h))
        def _(q=q):
            piece = piece_of(x, q)
            rcopy(piece, piece, f2_ssem.at[0, 0, q], f2_rsem.at[x, q], sibling).wait_recv()
            to_sibling(x, q)

        @pl.when(active)
        def _(q=q):
            for s in (1, 3, 2):
                xs = (x + s) % NX
                piece = piece_of(xs, q)
                rcopy(piece, piece, f2_ssem.at[0, 0, q], f2_rsem.at[xs, q], sibling).wait_recv()
                to_sibling(xs, q)

        @pl.when(jnp.logical_not(active))
        def _(q=q):
            for s in (0, 1, 3, 2):
                xs = (x + s) % NX
                piece = piece_of(xs, q)
                rcopy(piece, piece, f3_ssem.at[xs, q], f3_rsem.at[xs, q], sibling).wait_recv()
                emit(xs, q)

    @pl.when(root)
    def _():
        @pl.loop(1, NZ)
        def _(s):
            for q, rows in enumerate(GATHER):
                src, dst = w_mine.at[pl.ds(*rows)], w0_mine.at[pl.ds(*rows)]
                rcopy(src, dst, az_ssem.at[s, q], az_rsem.at[0, q], sibling).wait_send()

        for q in range(2):
            piece = piece_of(x, q)
            for s in range(4):
                for e in range(2):
                    if s or e:
                        rcopy(
                            piece, piece, f2_ssem.at[s, e, q], f2_rsem.at[x, q], sibling
                        ).wait_send()

    @pl.loop(1, NF)
    def _(s):
        rcopy(dsend, drecv.at[f], d_ssem.at[s], d_rsem.at[f], sibling).wait_send()
        for n in range(2):
            rcopy(
                att_out.at[n, f], att_in.at[n, f], c_ssem.at[n, s], c_rsem.at[n, f], sibling
            ).wait_send()
            rcopy(
                g_out.at[n, f], g_in.at[n, f], g_ssem.at[n, s], g_rsem.at[n, f], sibling
            ).wait_send()

    for s in range(1, 4):
        for q, rows in enumerate(GATHER):
            piece = w0_mine.at[pl.ds(*rows)]
            for j in range(2):
                rcopy(piece, piece, a1_ssem.at[j, s, q], a1_rsem.at[j, 0, q], sibling).wait_send()
                for k in range(4):
                    rcopy(
                        piece, piece, a2_ssem.at[j, s, k, q], a2_rsem.at[j, 0, 0, q], sibling
                    ).wait_send()
        for j, w in enumerate((t0.at[y], t1.at[x])):
            rcopy(w, w, b1_ssem.at[j, s], b1_rsem.at[j, 0], sibling).wait_send()
    for j in range(2):
        for k in range(4):
            block = m_in.at[j, k]
            rcopy(block, block, m_ssem.at[j, k], m_rsem.at[j, k], sibling).wait_send()
            for s in range(2):
                rcopy(block, block, b2_ssem.at[j, s, k], m_rsem.at[j, k], sibling).wait_send()
    att_copy.wait_send()
    c_copy.wait_send()
    g_copy.wait_send()
    for j in range(2):

        @pl.when(z != 4 * c + 2 * j + h)
        def _(j=j):
            for q, rows in enumerate(SPREAD):
                rows = pl.ds(*rows)
                rcopy(
                    vb.at[j, rows], zr.at[z, rows], bz_ssem.at[j, q], bz_rsem.at[z, q], sibling
                ).wait_send()

    @pl.when(active)
    def _():
        for s in range(4):
            for q in range(2):
                piece = piece_of(s, q)
                rcopy(piece, piece, f3_ssem.at[s, q], f3_rsem.at[s, q], sibling).wait_send()

    for out in outs:
        out.wait()
    for i in range(4):
        for q, rows in enumerate(SPREAD):
            pltpu.make_async_copy(
                piece_of(i, q),
                wg_hbm.at[pl.ds(*rows), QD * i : QD * (i + 1)],
                wg_sem.at[i, q],
            ).wait()


def finish(dq_in, dk_in, dv_in, wg_in, dq_out, dk_out, dv_out, wg_out, grads, wg_b, wg_f, sems):
    pairs = ((dq_in, dq_out), (dk_in, dk_out), (dv_in, dv_out))
    reads = [pltpu.make_async_copy(pairs[i][0], grads.at[i], sems.at[i]) for i in range(3)]
    reads.append(pltpu.make_async_copy(wg_in, wg_b, sems.at[3]))
    writes = [pltpu.make_async_copy(grads.at[i], pairs[i][1], sems.at[i]) for i in range(3)]
    writes.append(pltpu.make_async_copy(wg_f, wg_out, sems.at[3]))
    for read in reads:
        read.start()
    for i in range(3):
        reads[i].wait()
        writes[i].start()
    reads[3].wait()
    wg_f[...] = wg_b[...].astype(F32)
    for write in writes[3:]:
        write.start()
    for write in writes:
        write.wait()


def per_device(cotangent, out_weight, queries, key_vectors, value_vectors, destination, protein_ids):
    dma = pltpu.SemaphoreType.DMA
    vmem = pltpu.VMEM
    slots = jax.ShapeDtypeStruct((OWN, PAIRS * 128), BF16)
    any_space = pl.BlockSpec(memory_space=pl.ANY)
    in_vmem = pl.BlockSpec(memory_space=pltpu.VMEM)
    *grads, weight_grad = pl.pallas_call(
        kernel,
        out_shape=(slots, slots, slots, jax.ShapeDtypeStruct((ROWS, D), BF16)),
        in_specs=[any_space] * 5 + [in_vmem] * 2,
        out_specs=(any_space,) * 4,
        scratch_shapes=[
            *[vmem((OWN, PAIRS * 128), BF16) for _ in range(6)],
            vmem((8, TOK), jnp.int32),
            vmem((NF, 8, TOK), jnp.int32),
            vmem((2, TOK, D), BF16),
            vmem((NF * BLK, 5 * SPAD), BF16),
            vmem((NF * BLK, 5 * TOK), BF16),
            vmem((PAIRS, SPAD, 128), BF16),
            vmem((2, NF, BLK, 128), BF16),
            vmem((2, NF, BLK, 128), BF16),
            vmem((640, TOK), BF16),
            vmem((2, 640, TOK), BF16),
            vmem((PAIRS, 2 * OWN, OWN), F32),
            vmem((OWN, OWN), F32),
            vmem((NX, NY, ROWS, QD), BF16),
            vmem((NY, NX, ROWS, QD), BF16),
            vmem((2, 5, TOK, 128), BF16),
            vmem((5, TOK, 128), BF16),
            vmem((2, NF, BLK, 128), BF16),
            vmem((2, NF, BLK, 128), BF16),
            vmem((5, OWN, 128), BF16),
            *[vmem((4, 4, ROWS, QD), BF16) for _ in range(4)],
            *[vmem((2, 4, ROWS, QD), BF16) for _ in range(2)],
            *[vmem((4, ROWS, QD), BF16) for _ in range(4)],
            vmem((2, ROWS, QD), F32),
            vmem((2, ROWS, QD), BF16),
            vmem((NZ, ROWS, QD), BF16),
            vmem((NX, ROWS, QD), BF16),
            dma((4,)), dma((3,)), dma((4, 2)), dma((2,)),
            dma((NF,)), dma((NF,)), *[dma((2, NF)) for _ in range(4)],
            dma((NZ, 2)), dma((2, 2)), dma((2, 4, 2)), dma((2, 4, 2)),
            dma((2, 4, 4, 2)), dma((2, 4, 4, 2)),
            dma((3,)), dma((3,)),
            dma((2, 4)), dma((2, 4)), dma((2, 2, 4)), dma((2, 4, 4)),
            dma((2, 4)), dma((2, 4)), dma((2, 2)), dma((NZ, 2)),
            dma((4, 2, 2)), dma((4, 2)), dma((4, 2)), dma((4, 2)),
        ],
        compiler_params=pltpu.CompilerParams(
            collective_id=0, has_side_effects=True, vmem_limit_bytes=56 * 1024 * 1024
        ),
    )(
        cotangent, out_weight, queries, key_vectors, value_vectors,
        destination.reshape(1, TOK), protein_ids.reshape(1, OWN),
    )
    return pl.pallas_call(
        finish,
        out_shape=(slots, slots, slots, jax.ShapeDtypeStruct((ROWS, D), F32)),
        in_specs=[any_space] * 4,
        out_specs=(any_space,) * 4,
        scratch_shapes=[vmem((3, OWN, PAIRS * 128), BF16), vmem((ROWS, D), BF16), vmem((ROWS, D), F32), dma((4,))],
    )(*grads, weight_grad)


def solution(mesh):
    rows = P(("dp", "fsdp"), None)
    return jax.shard_map(
        per_device,
        mesh=mesh,
        in_specs=(rows, P("fsdp", None), rows, rows, rows, P(("dp", "fsdp")), P(("dp", "fsdp"))),
        out_specs=(rows, rows, rows, P("fsdp", None)),
        check_vma=False,
    )
```

```python
import jax
import jax.numpy as jnp
from jax import lax
from jax.experimental import pallas as pl
from jax.experimental.pallas import tpu as pltpu
from jax.sharding import PartitionSpec as P

F32 = jnp.float32
BF16 = jnp.bfloat16
MESH = pl.DeviceIdType.MESH

NX, NY, NZ, NF = 4, 4, 8, 16
TOK = 128
OWN = 192
CAP = 12
D = 2560
QD = D // 4
ROWS = 80
GATHER = ((0, 32), (32, 48))
SPREAD = ((0, 48), (48, 32))
BLK = 64
SPAD = 256
PAIRS = 10
SCALE = 0.125


def fdiv(values, by):
    return jnp.floor((values + 0.5) * (1.0 / by))


def iota(shape, dim):
    return lax.broadcasted_iota(jnp.int32, shape, dim).astype(F32)


def dot_nt(a, b):
    return lax.dot_general(a, b, (((1,), (1,)), ((), ())), preferred_element_type=F32)


def dot_tn(a, b):
    return lax.dot_general(a, b, (((0,), (0,)), ((), ())), preferred_element_type=F32)


def dot_nn(a, b):
    return jnp.dot(a, b, preferred_element_type=F32)


def row_of(y, j):
    return 4 * j + y


def kernel(
    cot_hbm, w_hbm, q_hbm, k_hbm, v_hbm, dest_ref, ids_ref,
    dq_hbm, dk_hbm, dv_hbm, wg_hbm,
    q_v, k_v, v_v, dq_v, dk_v, dv_v,
    dsend, drecv, c_all, h_own, h_tok,
    att, att_out, att_in, att_t, att_all, probs, same_v,
    w0, w1, g_tmp, g_tok, g_out, g_in, g_v,
    s0, s1, r0, r1, m_in, m_out, t0, t1, u0, u1, vf, vb, zr, fall,
    load_sem, out_sem, wg_sem, own_sem,
    d_ssem, d_rsem, c_ssem, c_rsem, g_ssem, g_rsem,
    az_ssem, az_rsem, a1_ssem, a1_rsem, a2_ssem, a2_rsem,
    sib_ssem, sib_rsem,
    m_ssem, m_rsem, b2_ssem, b2_rsem, b1_ssem, b1_rsem, bz_ssem, bz_rsem,
    f2_ssem, f2_rsem, f3_ssem, f3_rsem,
):
    dp = lax.axis_index("dp")
    f = lax.axis_index("fsdp")
    c = dp % 2
    x = (dp // 2) % NX
    h = dp // 8
    z = f // 2
    y = 2 * h + f % 2
    o = 1 - c

    def dev(x_, y_, z_, c_):
        return (((y_ // 2) * NX + x_) * 2 + c_, z_ * 2 + y_ % 2)

    def rcopy(src, dst, ssem, rsem, target):
        return pltpu.make_async_remote_copy(
            src_ref=src, dst_ref=dst, send_sem=ssem, recv_sem=rsem,
            device_id=target, device_id_type=MESH,
        )

    sibling = dev(x, y, z, o)

    loads = [
        pltpu.make_async_copy(src, dst, load_sem.at[i])
        for i, (src, dst) in enumerate(
            ((q_hbm, q_v), (k_hbm, k_v), (v_hbm, v_v), (cot_hbm, c_all.at[c]))
        )
    ]
    for load in loads:
        load.start()

    barrier = pltpu.get_barrier_semaphore()

    @pl.loop(1, NF)
    def _(s):
        pl.semaphore_signal(
            barrier, inc=1, device_id=(dp, (f + s) % NF), device_id_type=MESH
        )

    for s in range(1, 4):
        pl.semaphore_signal(
            barrier, inc=1, device_id=dev((x + s) % NX, y, z, c), device_id_type=MESH
        )
        pl.semaphore_signal(
            barrier, inc=1, device_id=dev(x, (y + s) % NY, z, c), device_id_type=MESH
        )
        pl.semaphore_signal(
            barrier, inc=1, device_id=dev((x + s) % NX, (y + 2) % NY, z, c), device_id_type=MESH
        )
    pl.semaphore_signal(barrier, inc=1, device_id=sibling, device_id_type=MESH)

    ids = ids_ref[...].astype(F32)
    srow = iota((OWN, OWN), 0)
    scol = iota((OWN, OWN), 1)
    ids_col = jnp.sum(
        jnp.where(srow == scol, jnp.broadcast_to(ids, (OWN, OWN)), 0.0), axis=1, keepdims=True
    )
    same_v[...] = jnp.where(ids_col == ids, 1.0, 0.0)
    dest = dest_ref[...]
    dsend[...] = jnp.broadcast_to(dest, (8, TOK))
    att[:, OWN:SPAD] = jnp.zeros((PAIRS, SPAD - OWN, 128), BF16)
    lane = lax.broadcasted_iota(jnp.int32, (1, 128), 1)
    head_masks = (
        jnp.where(lane < 64, 1.0, 0.0).astype(BF16),
        jnp.where(lane < 64, 0.0, 1.0).astype(BF16),
    )
    first_head = lax.broadcasted_iota(jnp.int32, (OWN, 128), 1) < 64

    def both_heads(rows):
        return jnp.concatenate([rows * head_masks[0], rows * head_masks[1]], axis=0)

    def forward(pairs):
        at = [pl.ds(pl.multiple_of(p * 128, 128), 128) for p in pairs]
        same = jnp.concatenate([same_v[...], same_v[...]], axis=0) > 0.0
        values = [v_v[:, a] for a in at]
        scores = [dot_nt(both_heads(q_v[:, a]), k_v[:, a]) * SCALE for a in at]
        scores = [jnp.where(same, t, -1e30) for t in scores]
        tops = [jnp.max(t, axis=1, keepdims=True) for t in scores]
        exps = [jnp.exp(t - top) for t, top in zip(scores, tops)]
        sums = [jnp.sum(e, axis=1, keepdims=True) for e in exps]
        prob = [e * (1.0 / t) for e, t in zip(exps, sums)]
        outs = [dot_nn(t.astype(BF16), v) for t, v in zip(prob, values)]
        for p, t, out in zip(pairs, prob, outs):
            probs[p] = t
            att[p, 0:OWN] = jnp.where(first_head, out[:OWN], out[OWN:]).astype(BF16)

    for load in loads[:3]:
        load.wait()
    forward([5 * o + i for i in range(2)])
    pl.semaphore_wait(barrier, 25)

    @pl.loop(1, NF)
    def _(s):
        rcopy(dsend, drecv.at[f], d_ssem.at[s], d_rsem.at[f], (dp, (f + s) % NF)).start()

    drecv[f] = dsend[...]

    active = z // 4 == c
    root = jnp.logical_and(active, z % 2 == h)
    root_j = (z % 4) // 2
    w_mine = w_hbm.at[:, pl.ds(pl.multiple_of(x * QD, 128), QD)]

    def spread_z(dst):
        for q, rows in enumerate(GATHER):
            src, to = w_mine.at[pl.ds(*rows)], dst.at[pl.ds(*rows)]
            pltpu.make_async_copy(src, to, own_sem.at[q]).start()

            @pl.loop(1, NZ)
            def _(s, q=q, src=src, to=to):
                rcopy(
                    src, to, az_ssem.at[s, q], az_rsem.at[root_j, q], dev(x, y, (z + s) % NZ, c)
                ).start()

    w0_mine = w0.at[x, y]
    w1_mine = w1.at[y, x]

    @pl.when(jnp.logical_and(root, root_j == 0))
    def _():
        spread_z(w0_mine)

    @pl.when(jnp.logical_and(root, root_j == 1))
    def _():
        spread_z(w1_mine)

    c_copy = rcopy(cot_hbm, c_all.at[c], sib_ssem.at[1], sib_rsem.at[1], sibling)
    c_copy.start()

    forward([5 * o + i for i in range(2, 5)])

    @pl.loop(1, NF)
    def _(s):
        frm = (f + s) % NF
        rcopy(dsend, drecv.at[frm], d_ssem.at[s], d_rsem.at[frm], sibling).wait_recv()

    row_i = iota((TOK, TOK), 0)
    col_i = iota((TOK, TOK), 1)
    p_col = iota((NF * BLK, 1), 0)
    p_dev = fdiv(p_col, BLK)
    p_in = p_col - p_dev * BLK
    p_pair = fdiv(p_in, CAP)
    p_rank = p_in - p_pair * CAP
    dests = jnp.concatenate([drecv[k][0:1] for k in range(NF)], axis=0).astype(F32)
    owners = fdiv(dests, OWN)
    here = owners == f.astype(F32)
    before = jnp.where(row_i < col_i, 1.0, 0.0).astype(BF16)
    ranks = dot_nn(jnp.where(here, 1.0, 0.0).astype(BF16), before)
    ranks = jnp.where(here, ranks, -1.0).astype(BF16)
    slots = (dests - owners * OWN).astype(BF16)
    source = jnp.where(p_dev == iota((NF * BLK, NF), 1), 1.0, 0.0).astype(BF16)
    slot_col = jnp.sum(
        jnp.where(dot_nn(source, ranks) == p_rank, dot_nn(source, slots) + 1.0, 0.0),
        axis=1, keepdims=True,
    )
    slot_lane = iota((1, SPAD), 1) + 1.0
    for k in range(5):
        h_own[:, SPAD * k : SPAD * (k + 1)] = jnp.where(
            jnp.where(p_pair == k, slot_col, 0.0) == slot_lane, 1.0, 0.0
        ).astype(BF16)

    def send_att(n, part):
        rows = att[pl.ds(5 * part, 5)].reshape(5 * SPAD, 128)
        att_out[n] = dot_nn(h_own[...], rows).astype(BF16).reshape(NF, BLK, 128)

        @pl.loop(1, NF)
        def _(s):
            to = (f + s) % NF
            rcopy(
                att_out.at[n, to], att_in.at[n, f], c_ssem.at[n, s], c_rsem.at[n, f], (dp, to)
            ).start()

        att_in[n, f] = att_out[n, f]

    send_att(0, o)


    def lane(j):
        if j == 0:
            return w0, x, y, lambda at: dev(at, y, z, c)
        return w1, y, x, lambda at: dev(x, at, z, c)

    def pass_on(j, k, q):
        ref, me, _, at = lane(j)
        piece = ref.at[me, k, pl.ds(*GATHER[q])]
        for s in (1, 3):
            rcopy(
                piece, piece, a2_ssem.at[j, s, k, q], a2_rsem.at[j, me, k, q], at((me + s) % 4)
            ).start()

    def relay(e):
        for q, rows in enumerate(GATHER):
            for j in range(2):
                ref, me, first, at = lane(j)
                k = (first + e) % 4
                ahead_by = 1 if e % 2 == 0 else 3
                behind = (me + 4 - ahead_by) % 4
                piece = ref.at[behind, k, pl.ds(*rows)]
                sems = a2_ssem.at[j, 2, k, q], a2_rsem.at[j, behind, k, q]
                rcopy(piece, piece, *sems, sibling).wait_recv()
                rcopy(piece, piece, *sems, at((me + ahead_by) % 4)).start()

    def begin(q):
        rows = pl.ds(*GATHER[q])

        @pl.when(root)
        def _():
            pltpu.make_async_copy(w_mine.at[rows], w0_mine.at[rows], own_sem.at[q]).wait()

        for j, mine in enumerate((w0_mine, w1_mine)):
            piece = mine.at[rows]

            @pl.when(z != 4 * c + 2 * j + h)
            def _(j=j, piece=piece):
                rcopy(piece, piece, az_ssem.at[0, q], az_rsem.at[j, q], sibling).wait_recv()

            me = y if j == 0 else x
            for s in (1, 3):
                to = dev(x, (y + s) % NY, z, c) if j == 0 else dev((x + s) % NX, y, z, c)
                rcopy(piece, piece, a1_ssem.at[j, s, q], a1_rsem.at[j, me, q], to).start()
            pass_on(j, me, q)

    begin(0)
    forward([5 * c + i for i in range(2)])
    begin(1)
    forward([5 * c + i for i in range(2, 5)])
    send_att(1, c)

    dest_f = dest.astype(F32)
    owner = fdiv(dest_f, OWN)
    owner_col = jnp.sum(
        jnp.where(row_i == col_i, jnp.broadcast_to(owner, (TOK, TOK)), 0.0),
        axis=1, keepdims=True,
    )
    ahead = jnp.where(jnp.logical_and(owner_col == owner, row_i < col_i), 1.0, 0.0)
    position = owner * CAP + jnp.sum(ahead, axis=0, keepdims=True)
    p_pos = p_dev * CAP + p_rank
    for k in range(5):
        h_tok[:, TOK * k : TOK * (k + 1)] = jnp.where(
            jnp.where(p_pair == k, p_pos, -1.0) == position, 1.0, 0.0
        ).astype(BF16)

    for s in (1, 3, 2):
        ys, xs = (y + s) % NY, (x + s) % NX
        for q, rows in enumerate(GATHER):
            for j, ref, k in ((0, w0.at[x, ys], ys), (1, w1.at[y, xs], xs)):
                piece = ref.at[pl.ds(*rows)]
                rcopy(piece, piece, a1_ssem.at[j, s, q], a1_rsem.at[j, k, q], sibling).wait_recv()
                if (s, q) in ((3, 0), (1, 1)):
                    to = dev(x, (y - s + 4) % NY, z, c) if j == 0 else dev((x - s + 4) % NX, y, z, c)
                    rcopy(piece, piece, a1_ssem.at[j, 2, q], a1_rsem.at[j, k, q], to).start()
                pass_on(j, k, q)

    relay(0)

    def take_att(n):
        @pl.loop(1, NF)
        def _(s):
            frm = (f + s) % NF
            rcopy(
                att_out.at[n, frm], att_in.at[n, frm], c_ssem.at[n, s], c_rsem.at[n, frm], sibling
            ).wait_recv()

        out = dot_tn(att_in[n].reshape(NF * BLK, 128), h_tok[...]).astype(BF16)
        return jnp.concatenate([out[:, TOK * k : TOK * (k + 1)] for k in range(5)], axis=0)

    att_t[...] = take_att(0)
    att_copy = rcopy(att_t, att_all.at[c], sib_ssem.at[0], sib_rsem.at[0], sibling)
    att_copy.start()
    relay(1)
    att_all[c] = take_att(1)
    relay(3)
    loads[3].wait()
    rcopy(cot_hbm, c_all.at[o], sib_ssem.at[1], sib_rsem.at[1], sibling).wait_recv()
    rcopy(att_t, att_all.at[o], sib_ssem.at[0], sib_rsem.at[0], sibling).wait_recv()

    def sums_lane(j):
        if j == 0:
            return s0, r0, x, y, lambda at: dev(at, y, z, c)
        return s1, r1, y, x, lambda at: dev(x, at, z, c)

    def far_out(j, e):
        own, _, me, first, at = sums_lane(j)
        k = (first + e) % 4
        ahead_by = 1 if e % 2 == 0 else 3
        rcopy(
            own.at[(me + 2) % 4, k], m_in.at[j, k], m_ssem.at[j, k], m_rsem.at[j, k],
            at((me + ahead_by) % 4),
        ).start()

    def near_out(j, e):
        own, ins, me, first, at = sums_lane(j)
        k = (first + e) % 4
        behind = (me + (3 if e % 2 == 0 else 1)) % 4
        rcopy(
            own.at[behind, k], ins.at[me, k], b2_ssem.at[j, 0, k], b2_rsem.at[j, me, k], at(behind)
        ).start()

    def sum_out(j, e):
        own, ins, me, first, at = sums_lane(j)
        k = (first + e) % 4
        to = (me + (1 if e % 2 == 0 else 3)) % 4
        rcopy(m_in.at[j, k], m_in.at[j, k], m_ssem.at[j, k], m_rsem.at[j, k], sibling).wait_recv()
        m_out[j, k] = (own[to, k].astype(F32) + m_in[j, k].astype(F32)).astype(BF16)
        rcopy(
            m_out.at[j, k], ins.at[me, k], b2_ssem.at[j, 1, k], b2_rsem.at[j, me, k], at(to)
        ).start()

    att_both = jnp.concatenate([att_all[0], att_all[1]], axis=1)
    for s in (2, 1, 3, 0):
        xs = (x + s) % NX
        cols = c_all[:, :, pl.ds(pl.multiple_of(xs * QD, 128), QD)].reshape(2 * TOK, QD)
        share = dot_nn(att_both, cols)
        for ys in range(NY):
            n = row_of(ys, 0)
            s0[xs, ys] = share[ROWS * n : ROWS * (n + 1)].astype(BF16)
            n = row_of(ys, 1)
            s1[ys, xs] = share[ROWS * n : ROWS * (n + 1)].astype(BF16)
        far_out(1, s)
        if s == 2:
            for e in (2, 1, 3, 0):
                far_out(0, e)
        if s % 2:
            for e in (2, 0) if s == 3 else (1, 3):
                near_out(0, e)
        near_out(1, s)
    relay(2)
    for e in (2, 1, 3, 0):
        for j in range(2):
            sum_out(j, e)

    for e in range(4):
        for j in range(2):
            ref, me, first, _ = lane(j)
            k = (first + e) % 4
            for s in (1 if e % 2 == 0 else 3, 2):
                for q, rows in enumerate(GATHER):
                    piece = ref.at[(me + s) % 4, k, pl.ds(*rows)]
                    rcopy(
                        piece, piece, a2_ssem.at[j, s, k, q], a2_rsem.at[j, (me + s) % 4, k, q],
                        sibling,
                    ).wait_recv()
    total = None
    for k in range(4):
        blocks = []
        for n in range(8):
            ys, j = n % 4, n // 4
            blocks.append(w0[k, ys] if j == 0 else w1[ys, k])
        wk = jnp.concatenate(blocks, axis=0)
        cols = c_all[:, :, QD * k : QD * (k + 1)].reshape(2 * TOK, QD)
        term = dot_nt(cols, wk)
        total = term if total is None else total + term
    total = total.astype(BF16)
    for g in range(2):
        for i in range(5):
            g_tmp[g, i] = total[TOK * g : TOK * (g + 1), 128 * i : 128 * (i + 1)]
    g_copy = rcopy(g_tmp.at[o], g_tok, sib_ssem.at[2], sib_rsem.at[2], sibling)
    g_copy.start()

    def send_grad(n, rows):
        g_out[n] = dot_nn(h_tok[...], rows.reshape(5 * TOK, 128)).astype(BF16).reshape(NF, BLK, 128)

        @pl.loop(1, NF)
        def _(s):
            to = (f + s) % NF
            rcopy(
                g_out.at[n, to], g_in.at[n, f], g_ssem.at[n, s], g_rsem.at[n, f], (dp, to)
            ).start()

        g_in[n, f] = g_out[n, f]

    send_grad(0, g_tmp[c])
    rcopy(g_tmp.at[o], g_tok, sib_ssem.at[2], sib_rsem.at[2], sibling).wait_recv()
    send_grad(1, g_tok[...])

    for e in (2, 1, 3, 0):
        for j in range(2):
            if j == 0:
                own, ins, out, nxt, me, k = s0, r0, t0, u0, x, (y + e) % NY
                after, to = y, dev(x, k, z, c)
            else:
                own, ins, out, nxt, me, k = s1, r1, t1, u1, y, (x + e) % NX
                after, to = x, dev(k, y, z, c)
            acc = own[me, k].astype(F32)
            for s in (1, 3):
                frm = (me + s) % 4
                rcopy(
                    own.at[frm, k], ins.at[frm, k], b2_ssem.at[j, 0, 0], b2_rsem.at[j, frm, k],
                    sibling,
                ).wait_recv()
                acc += ins[frm, k].astype(F32)
            if e:
                out[k] = acc.astype(BF16)
                rcopy(
                    out.at[k], nxt.at[after], b1_ssem.at[j, e], b1_rsem.at[j, after], to
                ).start()
            else:
                vf[j] = acc

    for j, (me, src, dst) in enumerate(((y, t0, u0), (x, t1, u1))):
        acc = vf[j]
        for s in range(1, 4):
            frm = (me + s) % 4
            rcopy(
                src.at[frm], dst.at[frm], b1_ssem.at[j, s], b1_rsem.at[j, frm], sibling
            ).wait_recv()
            acc += dst[frm].astype(F32)
        vf[j] = acc
        vb[j] = acc.astype(BF16)
        z_root = 4 * c + 2 * j + h

        @pl.when(z != z_root)
        def _(j=j, z_root=z_root):
            for q, rows in enumerate(SPREAD):
                rcopy(
                    vb.at[j, pl.ds(*rows)], zr.at[z, pl.ds(*rows)], bz_ssem.at[j, q],
                    bz_rsem.at[z, q], dev(x, y, z_root, c),
                ).start()

    def take_grad(n):
        @pl.loop(1, NF)
        def _(s):
            frm = (f + s) % NF
            rcopy(
                g_out.at[n, frm], g_in.at[n, frm], g_ssem.at[n, s], g_rsem.at[n, frm], sibling
            ).wait_recv()

        out = dot_tn(g_in[n].reshape(NF * BLK, 128), h_own[...])
        for k in range(5):
            g_v[k] = out[:, SPAD * k : SPAD * (k + 1)].T[:OWN].astype(BF16)

    live = ids_col >= 0.0
    halves = (slice(0, OWN), slice(OWN, 2 * OWN))

    def backward(part, places):
        pairs = [5 * part + i for i in places]
        at = [pl.ds(pl.multiple_of(p * 128, 128), 128) for p in pairs]
        grads = [g_v[i] for i in places]
        prob = [probs[p] for p in pairs]
        pgs = [dot_nt(both_heads(g), v_v[:, a]) for g, a in zip(grads, at)]
        deltas = [jnp.sum(t * pg, axis=1, keepdims=True) for t, pg in zip(prob, pgs)]
        sgs = [(t * (pg - d)).astype(BF16) for t, pg, d in zip(prob, pgs, deltas)]
        pbs = [t.astype(BF16) for t in prob]
        dqs = [dot_nn(sg, k_v[:, a]) for sg, a in zip(sgs, at)]
        dks = [[dot_tn(sg[r], q_v[:, a]) for r in halves] for sg, a in zip(sgs, at)]
        dvs = [[dot_tn(pb[r], g) for r in halves] for pb, g in zip(pbs, grads)]

        def put(ref, a, parts, scale):
            value = jnp.where(first_head, parts[0], parts[1]) * scale
            ref[:, a] = jnp.where(live, value, 0.0).astype(BF16)

        for a, dq, dk, dv in zip(at, dqs, dks, dvs):
            put(dq_v, a, (dq[:OWN], dq[OWN:]), SCALE)
            put(dk_v, a, dk, SCALE)
            put(dv_v, a, dv, 1.0)

    take_grad(0)
    backward(c, (0, 1))
    backward(c, (2, 3, 4))
    take_grad(1)
    backward(o, (0, 1))
    def piece_of(i, q):
        return fall.at[i, pl.ds(*SPREAD[q])]

    def emit(i, q):
        pltpu.make_async_copy(
            piece_of(i, q),
            wg_hbm.at[pl.ds(*SPREAD[q]), pl.ds(pl.multiple_of(i * QD, 128), QD)],
            wg_sem.at[i, q],
        ).start()

    def to_sibling(i, q):
        piece = piece_of(i, q)
        rcopy(piece, piece, f3_ssem.at[i, q], f3_rsem.at[i, q], sibling).start()
        emit(i, q)

    @pl.when(root)
    def _():
        for q, (top, count) in enumerate(SPREAD):
            acc = vf[root_j, top : top + count]
            for s in range(1, NZ):
                frm = (z + s) % NZ
                rows = pl.ds(top, count)
                rcopy(
                    vb.at[0, rows], zr.at[frm, rows], bz_ssem.at[0, q], bz_rsem.at[frm, q], sibling
                ).wait_recv()
                acc += zr[frm, top : top + count].astype(F32)
            fall[x, top : top + count] = acc.astype(BF16)
            piece = piece_of(x, q)
            for s in (1, 3, 2, 0):
                for e in (2, 0):
                    if s or e:
                        rcopy(
                            piece, piece, f2_ssem.at[s, e // 2, q], f2_rsem.at[x, q],
                            dev((x + s) % NX, (y + e) % NY, z, c),
                        ).start()
            to_sibling(x, q)

    backward(o, (2, 3, 4))
    outs = [
        pltpu.make_async_copy(src, dst, out_sem.at[i])
        for i, (src, dst) in enumerate(((dq_v, dq_hbm), (dk_v, dk_hbm), (dv_v, dv_hbm)))
    ]
    for out in outs:
        out.start()

    for q in range(2):

        @pl.when(jnp.logical_and(active, z % 2 != h))
        def _(q=q):
            piece = piece_of(x, q)
            rcopy(piece, piece, f2_ssem.at[0, 0, q], f2_rsem.at[x, q], sibling).wait_recv()
            to_sibling(x, q)

        @pl.when(active)
        def _(q=q):
            for s in (1, 3, 2):
                xs = (x + s) % NX
                piece = piece_of(xs, q)
                rcopy(piece, piece, f2_ssem.at[0, 0, q], f2_rsem.at[xs, q], sibling).wait_recv()
                to_sibling(xs, q)

        @pl.when(jnp.logical_not(active))
        def _(q=q):
            for s in (0, 1, 3, 2):
                xs = (x + s) % NX
                piece = piece_of(xs, q)
                rcopy(piece, piece, f3_ssem.at[xs, q], f3_rsem.at[xs, q], sibling).wait_recv()
                emit(xs, q)

    @pl.when(root)
    def _():
        @pl.loop(1, NZ)
        def _(s):
            for q, rows in enumerate(GATHER):
                src, dst = w_mine.at[pl.ds(*rows)], w0_mine.at[pl.ds(*rows)]
                rcopy(src, dst, az_ssem.at[s, q], az_rsem.at[0, q], sibling).wait_send()

        for q in range(2):
            piece = piece_of(x, q)
            for s in range(4):
                for e in range(2):
                    if s or e:
                        rcopy(
                            piece, piece, f2_ssem.at[s, e, q], f2_rsem.at[x, q], sibling
                        ).wait_send()

    @pl.loop(1, NF)
    def _(s):
        rcopy(dsend, drecv.at[f], d_ssem.at[s], d_rsem.at[f], sibling).wait_send()
        for n in range(2):
            rcopy(
                att_out.at[n, f], att_in.at[n, f], c_ssem.at[n, s], c_rsem.at[n, f], sibling
            ).wait_send()
            rcopy(
                g_out.at[n, f], g_in.at[n, f], g_ssem.at[n, s], g_rsem.at[n, f], sibling
            ).wait_send()

    for s in range(1, 4):
        for q, rows in enumerate(GATHER):
            piece = w0_mine.at[pl.ds(*rows)]
            for j in range(2):
                rcopy(piece, piece, a1_ssem.at[j, s, q], a1_rsem.at[j, 0, q], sibling).wait_send()
                for k in range(4):
                    rcopy(
                        piece, piece, a2_ssem.at[j, s, k, q], a2_rsem.at[j, 0, 0, q], sibling
                    ).wait_send()
        for j, w in enumerate((t0.at[y], t1.at[x])):
            rcopy(w, w, b1_ssem.at[j, s], b1_rsem.at[j, 0], sibling).wait_send()
    for j in range(2):
        for k in range(4):
            block = m_in.at[j, k]
            rcopy(block, block, m_ssem.at[j, k], m_rsem.at[j, k], sibling).wait_send()
            for s in range(2):
                rcopy(block, block, b2_ssem.at[j, s, k], m_rsem.at[j, k], sibling).wait_send()
    att_copy.wait_send()
    c_copy.wait_send()
    g_copy.wait_send()
    for j in range(2):

        @pl.when(z != 4 * c + 2 * j + h)
        def _(j=j):
            for q, rows in enumerate(SPREAD):
                rows = pl.ds(*rows)
                rcopy(
                    vb.at[j, rows], zr.at[z, rows], bz_ssem.at[j, q], bz_rsem.at[z, q], sibling
                ).wait_send()

    @pl.when(active)
    def _():
        for s in range(4):
            for q in range(2):
                piece = piece_of(s, q)
                rcopy(piece, piece, f3_ssem.at[s, q], f3_rsem.at[s, q], sibling).wait_send()

    for out in outs:
        out.wait()
    for i in range(4):
        for q, rows in enumerate(SPREAD):
            pltpu.make_async_copy(
                piece_of(i, q),
                wg_hbm.at[pl.ds(*rows), QD * i : QD * (i + 1)],
                wg_sem.at[i, q],
            ).wait()


def finish(dq_in, dk_in, dv_in, wg_in, dq_out, dk_out, dv_out, wg_out, grads, wg_b, wg_f, sems):
    whole = ((dq_in, dq_out), (dk_in, dk_out), (dv_in, dv_out))
    reads, writes = [], []
    for q, (top, count) in enumerate(SPREAD):
        rows = pl.ds(top, count)
        reads.append(pltpu.make_async_copy(wg_in.at[rows], wg_b.at[rows], sems.at[3, q]))
        writes.append(pltpu.make_async_copy(wg_f.at[rows], wg_out.at[rows], sems.at[3, q]))
    for q in range(2):
        rows = pl.ds(q * (OWN // 2), OWN // 2)
        for i, (src, dst) in enumerate(whole):
            held = grads.at[i, rows]
            reads.append(pltpu.make_async_copy(src.at[rows], held, sems.at[i, q]))
            writes.append(pltpu.make_async_copy(held, dst.at[rows], sems.at[i, q]))
    for read in reads:
        read.start()
    for n, (read, write) in enumerate(zip(reads, writes)):
        read.wait()
        if n < 2:
            top, count = SPREAD[n]
            wg_f[top : top + count] = wg_b[top : top + count].astype(F32)
        write.start()
    for write in writes:
        write.wait()


def per_device(cotangent, out_weight, queries, key_vectors, value_vectors, destination, protein_ids):
    dma = pltpu.SemaphoreType.DMA
    vmem = pltpu.VMEM
    slots = jax.ShapeDtypeStruct((OWN, PAIRS * 128), BF16)
    any_space = pl.BlockSpec(memory_space=pl.ANY)
    in_vmem = pl.BlockSpec(memory_space=pltpu.VMEM)
    *grads, weight_grad = pl.pallas_call(
        kernel,
        out_shape=(slots, slots, slots, jax.ShapeDtypeStruct((ROWS, D), BF16)),
        in_specs=[any_space] * 5 + [in_vmem] * 2,
        out_specs=(any_space,) * 4,
        scratch_shapes=[
            *[vmem((OWN, PAIRS * 128), BF16) for _ in range(6)],
            vmem((8, TOK), jnp.int32),
            vmem((NF, 8, TOK), jnp.int32),
            vmem((2, TOK, D), BF16),
            vmem((NF * BLK, 5 * SPAD), BF16),
            vmem((NF * BLK, 5 * TOK), BF16),
            vmem((PAIRS, SPAD, 128), BF16),
            vmem((2, NF, BLK, 128), BF16),
            vmem((2, NF, BLK, 128), BF16),
            vmem((640, TOK), BF16),
            vmem((2, 640, TOK), BF16),
            vmem((PAIRS, 2 * OWN, OWN), F32),
            vmem((OWN, OWN), F32),
            vmem((NX, NY, ROWS, QD), BF16),
            vmem((NY, NX, ROWS, QD), BF16),
            vmem((2, 5, TOK, 128), BF16),
            vmem((5, TOK, 128), BF16),
            vmem((2, NF, BLK, 128), BF16),
            vmem((2, NF, BLK, 128), BF16),
            vmem((5, OWN, 128), BF16),
            *[vmem((4, 4, ROWS, QD), BF16) for _ in range(4)],
            *[vmem((2, 4, ROWS, QD), BF16) for _ in range(2)],
            *[vmem((4, ROWS, QD), BF16) for _ in range(4)],
            vmem((2, ROWS, QD), F32),
            vmem((2, ROWS, QD), BF16),
            vmem((NZ, ROWS, QD), BF16),
            vmem((NX, ROWS, QD), BF16),
            dma((4,)), dma((3,)), dma((4, 2)), dma((2,)),
            dma((NF,)), dma((NF,)), *[dma((2, NF)) for _ in range(4)],
            dma((NZ, 2)), dma((2, 2)), dma((2, 4, 2)), dma((2, 4, 2)),
            dma((2, 4, 4, 2)), dma((2, 4, 4, 2)),
            dma((3,)), dma((3,)),
            dma((2, 4)), dma((2, 4)), dma((2, 2, 4)), dma((2, 4, 4)),
            dma((2, 4)), dma((2, 4)), dma((2, 2)), dma((NZ, 2)),
            dma((4, 2, 2)), dma((4, 2)), dma((4, 2)), dma((4, 2)),
        ],
        compiler_params=pltpu.CompilerParams(
            collective_id=0, has_side_effects=True, vmem_limit_bytes=56 * 1024 * 1024
        ),
    )(
        cotangent, out_weight, queries, key_vectors, value_vectors,
        destination.reshape(1, TOK), protein_ids.reshape(1, OWN),
    )
    return pl.pallas_call(
        finish,
        out_shape=(slots, slots, slots, jax.ShapeDtypeStruct((ROWS, D), F32)),
        in_specs=[any_space] * 4,
        out_specs=(any_space,) * 4,
        scratch_shapes=[vmem((3, OWN, PAIRS * 128), BF16), vmem((ROWS, D), BF16), vmem((ROWS, D), F32), dma((4, 2))],
    )(*grads, weight_grad)


def solution(mesh):
    rows = P(("dp", "fsdp"), None)
    return jax.shard_map(
        per_device,
        mesh=mesh,
        in_specs=(rows, P("fsdp", None), rows, rows, rows, P(("dp", "fsdp")), P(("dp", "fsdp"))),
        out_specs=(rows, rows, rows, P("fsdp", None)),
        check_vma=False,
    )
```
